32 devices in a mesh: row: 4 (over y, x), col: 8 (over z, core).
Axes of the slice: x: 2, y: 2, z: 4, core: 2. Of those that a mesh axis runs over, the one named last changes fastest.
Arguments:
- activations: bfloat16 [128, 320, 512], P('row', 'col'), may hold values from -6 to 6
- gain_first: bfloat16 [512], replicated, may hold values from 0.5 to 1.5
- shift_first: bfloat16 [512], replicated, may hold values from -1.5 to 1.5
- in_weight: bfloat16 [512, 1024], replicated, may hold values from -0.25 to 0.25
- conv_kernel: bfloat16 [7, 7, 992], replicated, may hold values from -2.5 to 2.5
- mix_first: bfloat16 [32, 64], replicated, may hold values from -1 to 1
- mix_second: bfloat16 [64, 128], replicated, may hold values from -0.75 to 0.75
- mix_third: bfloat16 [128, 256], replicated, may hold values from -0.5 to 0.5
- mix_fourth: bfloat16 [256, 512], replicated, may hold values from -0.375 to 0.375
- out_weight: bfloat16 [512, 512], replicated, may hold values from -0.25 to 0.25
- scale_mixer: bfloat16 [512], replicated, may hold values from 0.5 to 1.5
- gain_second: bfloat16 [512], replicated, may hold values from 0.5 to 1.5
- shift_second: bfloat16 [512], replicated, may hold values from -1.5 to 1.5
- up_weight: bfloat16 [512, 2048], replicated, may hold values from -0.25 to 0.25
- up_bias: bfloat16 [2048], replicated, may hold values from -2.5 to 2.5
- down_weight: bfloat16 [2048, 512], replicated, may hold values from -0.125 to 0.125
- scale_mlp: bfloat16 [512], replicated, may hold values from 0.5 to 1.5
- valid_pixels: int32 [128, 320], P('row', 'col'), may hold values from 0 to 1, as said below
- tile_images: int32 [4, 8], replicated, may hold values from 0 to 33, as said below
- cotangent: bfloat16 [128, 320, 512], P('row', 'col'), may hold values from -6 to 6
Outputs:
- outputs: bfloat16 [128, 320, 512], P('row', 'col')
- grad_input: bfloat16 [128, 320, 512], P('row', 'col')
- grad_gain_first: float32 [512], replicated
- grad_shift_first: float32 [512], replicated
- grad_in_weight: float32 [512, 1024], replicated
- grad_conv_kernel: float32 [7, 7, 992], replicated
- grad_mix_first: float32 [32, 64], replicated
- grad_mix_second: float32 [64, 128], replicated
- grad_mix_third: float32 [128, 256], replicated
- grad_mix_fourth: float32 [256, 512], replicated
- grad_out_weight: float32 [512, 512], replicated
- grad_scale_mixer: float32 [512], replicated
- grad_gain_second: float32 [512], replicated
- grad_shift_second: float32 [512], replicated
- grad_up_weight: float32 [512, 2048], replicated
- grad_up_bias: float32 [2048], replicated
- grad_down_weight: float32 [2048, 512], replicated
- grad_scale_mlp: float32 [512], replicated
The draws below stay inside these ranges and needn't reach their ends.
Inputs may be any that keep to these rules, and one draw needn't show every extreme that they name: `tile_images`: each image number covers a rectangle of whole tiles; image 0 covers every row of tiles and more than half of the columns of tiles, from the first. `valid_pixels`: in each image the pixels marked 1 form the top-left rectangle of its area, of three quarters or more of its height and width; image 0 has padding columns.
All inputs are finite; a program needn't handle non-finite values.
Results may differ from the reference program's by a relative error of at most 0.017.
Values may be sent and summed in bfloat16 or wider, within the bound.
No kernel may reach another device: no remote copies, remote signals or barrier semaphores. Data moves between devices by JAX's collectives and lax.ppermute only.
A program may use at most 192 MiB of HBM per device.

```python
import jax
import jax.numpy as jnp
from jax import lax

WIDTH = 512
FFN_WIDTH = 2048
GATE_WIDTH = 992
TILE_ROWS = 32
TILE_COLS = 40
GRID_ROWS = 128
GRID_COLS = 320
N_ROW = 4
N_COL = 8


def split_points(key):
    row_key, col_key = jax.random.split(key)
    cut_row = jax.random.randint(row_key, (), 1, N_ROW)
    cut_col = jax.random.randint(col_key, (), N_COL // 2 + 1, N_COL)
    return (cut_row, cut_col)


def image_numbers(cut_row, cut_col, tile_row, tile_col):
    alone = 2 + tile_row * N_COL + tile_col
    return jnp.where(tile_col < cut_col, 0, jnp.where(tile_row < cut_row, 1, alone)).astype(jnp.int32)


def draw_tile_images(key, part):
    cut_row, cut_col = split_points(key)
    tile_row = jnp.arange(N_ROW, dtype=jnp.int32)[:, None]
    tile_col = jnp.arange(N_COL, dtype=jnp.int32)[None, :]
    return image_numbers(cut_row, cut_col, tile_row, tile_col)


def draw_valid_pixels(key, part):
    cut_row, cut_col = split_points(key)
    key = jax.random.fold_in(key, 7)
    row_key, col_key = jax.random.split(key)
    pixel_row = jnp.arange(GRID_ROWS, dtype=jnp.int32)[:, None]
    pixel_col = jnp.arange(GRID_COLS, dtype=jnp.int32)[None, :]
    tile_row = pixel_row // TILE_ROWS
    tile_col = pixel_col // TILE_COLS
    number = image_numbers(cut_row, cut_col, tile_row, tile_col)
    large = tile_col < cut_col
    upper = jnp.logical_and(jnp.logical_not(large), tile_row < cut_row)
    shared = jnp.logical_or(large, upper)
    top_row = jnp.where(shared, 0, tile_row * TILE_ROWS)
    left_col = jnp.where(large, 0, jnp.where(upper, cut_col * TILE_COLS, tile_col * TILE_COLS))
    height = jnp.where(large, GRID_ROWS, jnp.where(upper, cut_row * TILE_ROWS, TILE_ROWS))
    breadth = jnp.where(large, cut_col * TILE_COLS, jnp.where(upper, (N_COL - cut_col) * TILE_COLS, TILE_COLS))
    images = 2 + N_ROW * N_COL
    row_draw = jax.random.randint(row_key, (images,), 0, 1000)
    col_draw = jax.random.randint(col_key, (images,), 0, 1000)
    row_pad = height * row_draw[number] // 4000
    col_pad = breadth * col_draw[number] // 4000
    col_pad = jnp.where(number == 0, jnp.maximum(col_pad, 1), col_pad)
    inside = jnp.logical_and(pixel_row - top_row < height - row_pad, pixel_col - left_col < breadth - col_pad)
    return inside.astype(jnp.int32)


def levels(rng, dims, cuts, least, largest):
    gain = 1.0
    for axis_at, parts in cuts:
        heights = jax.random.uniform(jax.random.fold_in(jax.random.fold_in(rng, 6), axis_at), (parts,), jnp.float32, least / len(cuts), largest / len(cuts))
        gain = gain * jnp.repeat(jnp.exp(heights), dims[axis_at] // parts).reshape((-1,) + (1,) * (len(dims) - 1 - axis_at))
    return gain


def gaussian(stream_key, dims, deviation, reach, shards=(), kind=jnp.bfloat16):
    entries = jax.random.normal(stream_key, dims, jnp.float32) * deviation
    if len(shards) > 0:
        entries = levels(stream_key, dims, shards, -0.22, 0.18) * entries
    return jnp.clip(entries, min=-reach, max=reach).astype(kind)


def setup_inputs(seed: int = 0) -> dict:
    key_of = jax.random.split(jax.random.key(seed), 21)
    return {
        "activations": gaussian(key_of[0], (GRID_ROWS, GRID_COLS, WIDTH), 1.0, 6.0, ((0, 4), (1, 8))),
        "gain_first": jnp.clip(1.0 + 0.1 * jax.random.normal(key_of[1], (WIDTH,), jnp.float32), 0.5, 1.5).astype(jnp.bfloat16),
        "shift_first": gaussian(key_of[2], (WIDTH,), 0.3, 1.5),
        "in_weight": gaussian(key_of[3], (WIDTH, 2 * WIDTH), WIDTH ** -0.5, 0.25),
        "conv_kernel": gaussian(key_of[4], (7, 7, GATE_WIDTH), 5 ** -0.5, 2.5),
        "mix_first": gaussian(key_of[5], (WIDTH // 16, WIDTH // 8), (WIDTH // 16) ** -0.5, 1.0),
        "mix_second": gaussian(key_of[6], (WIDTH // 8, WIDTH // 4), (WIDTH // 8) ** -0.5, 0.75),
        "mix_third": gaussian(key_of[7], (WIDTH // 4, WIDTH // 2), (WIDTH // 4) ** -0.5, 0.5),
        "mix_fourth": gaussian(key_of[8], (WIDTH // 2, WIDTH), (WIDTH // 2) ** -0.5, 0.375),
        "out_weight": gaussian(key_of[9], (WIDTH, WIDTH), WIDTH ** -0.5, 0.25),
        "scale_mixer": jnp.clip(jax.random.uniform(key_of[10], (WIDTH,), jnp.float32, 0.5, 1.5), 0.5, 1.5).astype(jnp.bfloat16),
        "gain_second": jnp.clip(1.0 + 0.1 * jax.random.normal(key_of[11], (WIDTH,), jnp.float32), 0.5, 1.5).astype(jnp.bfloat16),
        "shift_second": gaussian(key_of[12], (WIDTH,), 0.3, 1.5),
        "up_weight": gaussian(key_of[13], (WIDTH, FFN_WIDTH), WIDTH ** -0.5, 0.25),
        "up_bias": gaussian(key_of[14], (FFN_WIDTH,), 0.5, 2.5),
        "down_weight": gaussian(key_of[15], (FFN_WIDTH, WIDTH), FFN_WIDTH ** -0.5, 0.125),
        "scale_mlp": jnp.clip(jax.random.uniform(key_of[16], (WIDTH,), jnp.float32, 0.5, 1.5), 0.5, 1.5).astype(jnp.bfloat16),
        "valid_pixels": draw_valid_pixels(jax.random.fold_in(key_of[20], 71), 0),
        "tile_images": draw_tile_images(jax.random.fold_in(key_of[20], 71), 0),
        "cotangent": gaussian(key_of[19], (GRID_ROWS, GRID_COLS, WIDTH), 1.0, 6.0, ((0, 4), (1, 8))),
    }


@jax.custom_vjp
def low(v):
    return lax.optimization_barrier(v.astype(jnp.bfloat16)).astype(jnp.float32)

@jax.custom_vjp
def low_back(v):
    return v

def low_keep(v):
    return (low(v), None)

def low_pass(kept, grad):
    return (grad,)

def back_keep(v):
    return (v, None)

def back_low(kept, grad):
    return (low(grad),)
low.defvjp(low_keep, low_pass)
low_back.defvjp(back_keep, back_low)
EPS = 1e-06
DW_SCALE = 1.0 / 3.0

def product(left, right):
    return jnp.dot(left, right, precision=lax.Precision.HIGHEST, preferred_element_type=jnp.float32)

def norm_pixels(values, gain_vec, shift_vec, validity):
    center = values - lax.optimization_barrier(jnp.mean(values, axis=-1, keepdims=True))
    inverse = lax.rsqrt(lax.optimization_barrier(jnp.mean(center * center, axis=-1, keepdims=True)) + EPS)
    return validity * (center * inverse * gain_vec + shift_vec)

def section_in(window, validity, gain_vec, shift_vec, in_weight):
    normed = low(norm_pixels(window, gain_vec, shift_vec, validity))
    joined = low_back(product(normed, in_weight))
    return (joined[..., :WIDTH // 16], low(joined[..., WIDTH // 16:]))

def depthwise(gate_ext, kernel, tile_rows, tile_cols):
    summed = jnp.zeros((tile_rows, tile_cols, gate_ext.shape[-1]), jnp.float32)
    for row_off in range(7):
        for col_off in range(7):
            summed = summed + kernel[row_off, col_off] * gate_ext[row_off:row_off + tile_rows, col_off:col_off + tile_cols]
    return DW_SCALE * summed

def section_out(gate_ext, lead_vals, inputs, params, validity, edge_mask):
    kernel = params[0]
    mixes = params[1:5]
    out_weight, scale_mixer, gain_second, shift_second, up_weight, up_bias, down_weight, scale_mlp = params[5:]
    spread = low_back(depthwise(gate_ext * edge_mask[..., None], kernel, inputs.shape[0], inputs.shape[1]))
    bounds = [0]
    for weight in mixes:
        bounds.append(bounds[-1] + weight.shape[0])
    bounds.append(bounds[-1] + mixes[-1].shape[1])
    mixed = lead_vals * spread[..., bounds[0]:bounds[1]]
    for section, weight in enumerate(mixes):
        mixed = low_back(product(low(mixed), weight)) * spread[..., bounds[section + 1]:bounds[section + 2]]
    branch = low_back(product(low(mixed), out_weight))
    middle = inputs + scale_mixer * branch
    normed = low(norm_pixels(middle, gain_second, shift_second, validity))
    pre_act = low_back(product(normed, up_weight) + up_bias)
    active = low(jax.nn.gelu(pre_act, approximate=False))
    return middle + scale_mlp * low_back(product(active, down_weight))

def assemble(tiles):
    depth = tiles.shape[-1]
    grid = tiles.reshape(N_ROW, N_COL, TILE_ROWS, TILE_COLS, depth)
    return grid.transpose(0, 2, 1, 3, 4).reshape(GRID_ROWS, GRID_COLS, depth)

def reference(activations, gain_first, shift_first, in_weight, conv_kernel, mix_first, mix_second, mix_third, mix_fourth, out_weight, scale_mixer, gain_second, shift_second, up_weight, up_bias, down_weight, scale_mlp, valid_pixels, tile_images, cotangent):
    inputs = activations.astype(jnp.float32)
    grad_out = cotangent.astype(jnp.float32)
    validity = valid_pixels.astype(jnp.float32)[..., None]
    padded_in = jnp.pad(inputs, ((3, 3), (3, 3), (0, 0)))
    padded_valid = jnp.pad(validity, ((3, 3), (3, 3), (0, 0)))
    owners = jnp.repeat(jnp.repeat(tile_images, TILE_ROWS, axis=0), TILE_COLS, axis=1)
    padded_owner = jnp.pad(owners, 3, constant_values=-1)
    first = tuple((param.astype(jnp.float32) for param in (gain_first, shift_first, in_weight)))
    second = tuple((param.astype(jnp.float32) for param in (conv_kernel, mix_first, mix_second, mix_third, mix_fourth, out_weight, scale_mixer, gain_second, shift_second, up_weight, up_bias, down_weight, scale_mlp)))
    gate_count = conv_kernel.shape[-1]
    span_rows = TILE_ROWS + 6
    span_cols = TILE_COLS + 6

    def tile_forward(carry, tile_index):
        grad_gates, totals = carry
        tile_row = (tile_index // N_COL).astype(jnp.int32)
        tile_col = (tile_index % N_COL).astype(jnp.int32)
        top_row = (tile_row * TILE_ROWS).astype(jnp.int32)
        left_col = (tile_col * TILE_COLS).astype(jnp.int32)
        zero_index = jnp.zeros((), jnp.int32)
        window = lax.dynamic_slice(padded_in, (top_row, left_col, zero_index), (span_rows, span_cols, WIDTH))
        valid_window = lax.dynamic_slice(padded_valid, (top_row, left_col, zero_index), (span_rows, span_cols, 1))
        owner_window = lax.dynamic_slice(padded_owner, (top_row, left_col), (span_rows, span_cols))
        own_image = tile_images[tile_row, tile_col]
        edge_mask = (owner_window == own_image).astype(jnp.float32)
        lead_window, gate_window = section_in(window, valid_window, *first)
        valid_center = valid_window[3:-3, 3:-3]
        grad_center = lax.dynamic_slice(grad_out, (top_row, left_col, zero_index), (TILE_ROWS, TILE_COLS, WIDTH))

        def forward_tile(gate_ext, lead_vals, center, params):
            return section_out(gate_ext, lead_vals, center, params, valid_center, edge_mask)
        result, pullback = jax.vjp(forward_tile, gate_window, lead_window[3:-3, 3:-3], window[3:-3, 3:-3], second)
        grad_gate_window, grad_lead, grad_center_in, grad_params = pullback(grad_center)
        previous = lax.dynamic_slice(grad_gates, (top_row, left_col, zero_index), (span_rows, span_cols, gate_count))
        grad_gates = lax.dynamic_update_slice(grad_gates, previous + grad_gate_window, (top_row, left_col, zero_index))
        totals = jax.tree.map(jnp.add, totals, grad_params)
        return ((grad_gates, totals), (result, grad_center_in, grad_lead))
    tile_count = N_ROW * N_COL
    start = (jnp.zeros((GRID_ROWS + 6, GRID_COLS + 6, gate_count), jnp.float32), jax.tree.map(jnp.zeros_like, second))
    (grad_gates, second_totals), (result_tiles, input_tiles, lead_tiles) = lax.scan(tile_forward, start, jnp.arange(tile_count, dtype=jnp.int32))
    grad_gates = grad_gates[3:3 + GRID_ROWS, 3:3 + GRID_COLS]
    grad_lead = assemble(lead_tiles)

    def tile_back(totals, tile_index):
        tile_row = (tile_index // N_COL).astype(jnp.int32)
        tile_col = (tile_index % N_COL).astype(jnp.int32)
        top_row = (tile_row * TILE_ROWS).astype(jnp.int32)
        left_col = (tile_col * TILE_COLS).astype(jnp.int32)
        zero_index = jnp.zeros((), jnp.int32)
        center = lax.dynamic_slice(inputs, (top_row, left_col, zero_index), (TILE_ROWS, TILE_COLS, WIDTH))
        valid_center = lax.dynamic_slice(validity, (top_row, left_col, zero_index), (TILE_ROWS, TILE_COLS, 1))
        lead_center = lax.dynamic_slice(grad_lead, (top_row, left_col, zero_index), (TILE_ROWS, TILE_COLS, WIDTH // 16))
        gate_center = lax.dynamic_slice(grad_gates, (top_row, left_col, zero_index), (TILE_ROWS, TILE_COLS, gate_count))

        def input_tile(values, gain_vec, shift_vec, weight):
            return section_in(values, valid_center, gain_vec, shift_vec, weight)
        unused_value, pullback = jax.vjp(input_tile, center, *first)
        grad_values, grad_gain, grad_shift, grad_weight = pullback((lead_center, gate_center))
        totals = jax.tree.map(jnp.add, totals, (grad_gain, grad_shift, grad_weight))
        return (totals, grad_values)
    first_totals, first_tiles = lax.scan(tile_back, jax.tree.map(jnp.zeros_like, first), jnp.arange(tile_count, dtype=jnp.int32))
    outputs = assemble(result_tiles).astype(jnp.bfloat16)
    grad_input = (assemble(input_tiles) + assemble(first_tiles)).astype(jnp.bfloat16)
    return (outputs, grad_input, first_totals[0], first_totals[1], first_totals[2], second_totals[0], second_totals[1], second_totals[2], second_totals[3], second_totals[4], second_totals[5], second_totals[6], second_totals[7], second_totals[8], second_totals[9], second_totals[10], second_totals[11], second_totals[12])
```

```python
import math
from functools import partial

import jax
import jax.numpy as jnp
import ml_dtypes
import numpy as np
from jax import lax
from jax.experimental import pallas as pl
from jax.experimental.pallas import tpu as pltpu
from jax.sharding import PartitionSpec as P

EPS = 1e-06
TAPS = 7
HALO = 3
OUT = 8
WIN = OUT + TAPS - 1
PITCH = 16
SLOTS = 112
OUTSIDE = 64.0
COS_SCALE = 1.422015
SIN_SCALE = 1.818765
TILES = 5
LANES = 512
BF16 = jnp.bfloat16
F32 = jnp.float32


def frequencies():
    pairs, own, seen = [], [], set()
    for u in range(WIN):
        for v in range(WIN):
            if (u, v) in seen:
                continue
            twin = ((-u) % WIN, (-v) % WIN)
            seen.update([(u, v), twin])
            (own if twin == (u, v) else pairs).append((u, v))
    return np.array(pairs + own), np.array([2.0] * len(pairs) + [1.0] * len(own))


def angles(rows, cols, pitch):
    freq, _ = frequencies()
    a = np.arange(rows)[:, None]
    b = np.arange(pitch)[None, :]
    theta = 2 * np.pi * (freq[:, 0, None, None] * a + freq[:, 1, None, None] * b) / WIN
    live = np.broadcast_to(b < cols, (rows, pitch))
    cos = np.zeros((SLOTS, rows * pitch))
    sin = np.zeros((SLOTS, rows * pitch))
    cos[: len(freq)] = (np.cos(theta) * live).reshape(len(freq), -1)
    sin[: len(freq)] = (np.sin(theta) * live).reshape(len(freq), -1)
    return cos, sin


def tables():
    _, weight = frequencies()
    weight = np.concatenate([weight, np.zeros(SLOTS - len(weight))])[:, None]
    area = WIN * WIN

    def ahead(cos, sin):
        return np.concatenate([COS_SCALE * cos, -SIN_SCALE * sin])

    def back(cos, sin):
        return np.concatenate([weight * COS_SCALE * cos, -weight * SIN_SCALE * sin]).T

    window = angles(WIN, WIN, PITCH)
    tile = angles(OUT, OUT, OUT)
    cos, sin = angles(TAPS, TAPS, TAPS)
    third = 1.0 / 3.0
    spectrum = np.concatenate(
        [
            cos * (third / (area * COS_SCALE**2)),
            -sin * (third / (area * COS_SCALE * SIN_SCALE)),
            cos * (third / (area * SIN_SCALE**2)),
        ]
    )
    wide = weight * third / area
    kernel_back = np.concatenate(
        [
            wide * cos / COS_SCALE**2,
            wide * cos / SIN_SCALE**2,
            -wide * sin / (COS_SCALE * SIN_SCALE),
            wide * sin / (COS_SCALE * SIN_SCALE),
        ]
    ).T
    kernel_back = np.concatenate([kernel_back, np.zeros((7, 4 * SLOTS))])
    half = ml_dtypes.bfloat16
    return dict(
        window=ahead(*window).astype(half),
        tile=ahead(*tile).astype(half),
        window_back=back(*window).astype(half),
        tile_back=back(*tile).astype(half),
        spectrum=np.concatenate([spectrum, spectrum[:, ::-1]]).astype(np.float32),
        kernel_back=kernel_back.astype(np.float32),
    )


def dot(left, right):
    return jnp.dot(left, right, preferred_element_type=F32)


def dot_right(left, right):
    return lax.dot_general(left, right, (((1,), (1,)), ((), ())), preferred_element_type=F32)


def dot_left(left, right):
    return lax.dot_general(left, right, (((0,), (0,)), ((), ())), preferred_element_type=F32)


def normalize(values):
    center = values - jnp.mean(values, axis=-1, keepdims=True)
    inverse = lax.rsqrt(jnp.mean(center * center, axis=-1, keepdims=True) + EPS)
    return center * inverse, inverse


def norm_back(masked, normal, inverse, gain):
    scaled = masked * gain
    centered = scaled - jnp.mean(scaled, axis=-1, keepdims=True)
    return inverse * (centered - normal * jnp.mean(scaled * normal, axis=-1, keepdims=True))


def gelu_pair(x):
    cumulative = 0.5 + 0.5 * lax.erf(x * math.sqrt(0.5))
    density = jnp.exp(-0.5 * x * x) * (1.0 / math.sqrt(2.0 * math.pi))
    return x * cumulative, cumulative + x * density


def depthwise(ext, first_row, spec, tx, ty, waves, mixed_waves, result_ref, kept=None):
    span = 48

    def block_of_lanes(block, carry):
        lanes = pl.ds(pl.multiple_of(LANES * block, LANES), LANES)
        window = jnp.concatenate(
            [
                jnp.concatenate(
                    [
                        ext[pl.ds(pl.multiple_of((first_row + r) * span + OUT * col, 8), PITCH), lanes]
                        for r in range(WIN)
                    ],
                    axis=0,
                ).astype(BF16)
                for col in range(TILES)
            ],
            axis=1,
        )
        waves[...] = dot(tx[...], window)
        for row in range(0, SLOTS, 16):
            here, there = slice(row, row + 16), slice(SLOTS + row, SLOTS + row + 16)
            low, cross, high = (spec[pl.ds(SLOTS * k + row, 16), lanes] for k in range(3))
            for col in range(TILES):
                at = slice(LANES * col, LANES * col + LANES)
                real, imag = waves[here, at], waves[there, at]
                mixed_waves[here, at] = (low * real + cross * imag).astype(BF16)
                mixed_waves[there, at] = (high * imag - cross * real).astype(BF16)
                if kept is not None:
                    base = 2 * SLOTS * col + row
                    kept[base : base + 16, lanes] = real.astype(BF16)
                    kept[base + SLOTS : base + SLOTS + 16, lanes] = imag.astype(BF16)
        result = dot(ty[...], mixed_waves[...])
        for col in range(TILES):
            for r in range(OUT):
                result_ref[r * 40 + OUT * col : r * 40 + OUT * col + OUT, lanes] = result[
                    OUT * r : OUT * r + OUT, LANES * col : LANES * col + LANES
                ]
        return carry

    lax.fori_loop(0, 1024 // LANES, block_of_lanes, 0)


GAIN_1, SHIFT_1, SCALE_1, GAIN_2, SHIFT_2, SCALE_2 = range(6)


def forward_kernel(
    x_ext, x_own, valid, cot, vecs, up_bias, in_w, w1, w2, w3, w4, out_w, up_w, spec, tx, ty,
    waves_out, spread, prods, lead_out, middle_out, active_out, slope_out, grad_down,
    ext, waves, mixed_waves, active_all, gdown_all,
):
    step = pl.program_id(0)
    span = 48
    chunk = spread.shape[0]
    gain = vecs[GAIN_1 : GAIN_1 + 1, :]
    shift = vecs[SHIFT_1 : SHIFT_1 + 1, :]

    def project(start, rows):
        at = pl.ds(start, rows)
        values = x_ext[at, :].astype(F32)
        normal, _ = normalize(values)
        normed = jnp.where(values[:, :1] < 0.5 * OUTSIDE, normal * gain + shift, 0.0).astype(BF16)
        for block in range(2):
            lanes = slice(512 * block, 512 * block + 512)
            joined = dot(normed, in_w[:, lanes])
            if block == 0:
                ext[at, 1024:1152] = joined[:, :128]
            low = joined.astype(BF16)
            ext[at, lanes] = low.astype(F32)

    @pl.when(step == 0)
    def _():
        project(0, 6 * span)

    project(pl.multiple_of((OUT * step + 6) * span, 16), OUT * span)

    depthwise(ext, OUT * step, spec, tx, ty, waves, mixed_waves, spread, waves_out)

    lead = jnp.concatenate(
        [
            ext[pl.ds(pl.multiple_of((OUT * step + HALO + r) * span, 8), span), 1024:1152][HALO : HALO + 40]
            for r in range(OUT)
        ],
        axis=0,
    )
    lead = pltpu.roll(lead, 32, 1)
    lead_out[...] = lead
    mixed = lead * spread[:, :128]
    for weight, lo, hi in ((w1, 0, 128), (w2, 128, 256), (w3, 256, 512), (w4, 512, 1024)):
        produced = dot(mixed.astype(BF16), weight[...])
        prods[:, lo:hi] = produced
        mixed = produced * spread[:, lo:hi]
    branch = dot(mixed.astype(BF16), out_w[...])
    middle = x_own[...].astype(F32) + vecs[SCALE_1 : SCALE_1 + 1, :] * branch
    middle_out[...] = middle
    normal, _ = normalize(middle)
    normed = (
        (normal * vecs[GAIN_2 : GAIN_2 + 1, :] + vecs[SHIFT_2 : SHIFT_2 + 1, :]) * valid[...]
    ).astype(BF16)
    rows = pl.ds(pl.multiple_of(step * chunk, 16), chunk)
    for block in range(4):
        lanes = slice(512 * block, 512 * block + 512)
        pre = dot(normed, up_w[:, lanes]) + up_bias[:, lanes]
        active, slope = gelu_pair(pre)
        active = active.astype(BF16)
        active_out[:, lanes] = active
        active_all[rows, lanes] = active
        slope_out[:, lanes] = slope.astype(BF16)
    gdown_all[rows, :] = (cot[...].astype(F32) * vecs[SCALE_2 : SCALE_2 + 1, :]).astype(BF16)

    @pl.when(step == pl.num_programs(0) - 1)
    def _():
        for block in range(4):
            lanes = slice(512 * block, 512 * block + 512)
            grad_down[lanes, :] = dot_left(gdown_all[...], active_all[:, lanes]).astype(BF16)


def ffn_back_kernel(
    cot, slope, middle, valid, vecs, down_w, up_w, grad_down,
    gmiddle, sent, kept, vec_sums, bias_sum,
    normed_all, gpre_all,
):
    step = pl.program_id(0)
    chunk = cot.shape[0]
    rows = pl.ds(pl.multiple_of(step * chunk, 16), chunk)

    @pl.when(step == 0)
    def _():
        vec_sums[...] = jnp.zeros_like(vec_sums)
        bias_sum[...] = jnp.zeros_like(bias_sum)

    grad = cot[...].astype(F32)
    gdown = (grad * vecs[SCALE_2 : SCALE_2 + 1, :]).astype(BF16)
    gnormed = jnp.zeros((chunk, 512), F32)
    for block in range(4):
        lanes = slice(512 * block, 512 * block + 512)
        gactive = dot_right(gdown, down_w[lanes, :])
        gpre = (gactive * slope[:, lanes].astype(F32)).astype(BF16)
        gpre_all[rows, lanes] = gpre
        bias_sum[0:1, lanes] += jnp.sum(gpre.astype(F32), axis=0, keepdims=True)
        gnormed = gnormed + dot_right(gpre, up_w[:, lanes])
    normal, inverse = normalize(middle[...])
    gain = vecs[GAIN_2 : GAIN_2 + 1, :]
    mask = valid[...]
    normed_all[rows, :] = ((normal * gain + vecs[SHIFT_2 : SHIFT_2 + 1, :]) * mask).astype(BF16)
    masked = gnormed * mask
    vec_sums[0:1, :] += jnp.sum(masked * normal, axis=0, keepdims=True)
    vec_sums[1:2, :] += jnp.sum(masked, axis=0, keepdims=True)
    gmiddle[...] = grad + norm_back(masked, normal, inverse, gain)

    @pl.when(step == pl.num_programs(0) - 1)
    def _():
        def finish(for_up, for_down):
            for block in range(4):
                lanes = slice(512 * block, 512 * block + 512)
                for_up[lanes, :] = dot_left(normed_all[...], gpre_all[:, lanes]).astype(BF16)
            for_down[...] = grad_down[...]

        even = lax.axis_index("col") % 2 == 0
        pl.when(even)(lambda: finish(sent, kept))
        pl.when(jnp.logical_not(even))(lambda: finish(kept, sent))


def mixer_back_kernel(
    gmiddle, spread, prods, lead, vecs, w1, w2, w3, w4, out_w,
    gspread, glead, grads,
    d_out, d_4, d_3, d_2, d_1,
):
    step = pl.program_id(0)

    @pl.when(step == 0)
    def _():
        for total in (d_out, d_4, d_3, d_2, d_1):
            total[...] = jnp.zeros_like(total)

    grad = gmiddle[...]
    glow = (grad * vecs[SCALE_1 : SCALE_1 + 1, :]).astype(BF16)
    part, prod = spread[:, 512:1024], prods[:, 512:1024]
    d_out[...] += dot_left((prod * part).astype(BF16), glow)
    gmixed = dot_right(glow, out_w[...])
    for weight, total, lo, hi, below in (
        (w4, d_4, 512, 1024, 256), (w3, d_3, 256, 512, 128), (w2, d_2, 128, 256, 0)
    ):
        gspread[:, lo:hi] = (gmixed * prods[:, lo:hi]).astype(BF16)
        gprod = (gmixed * spread[:, lo:hi]).astype(BF16)
        mixed = (prods[:, below:lo] * spread[:, below:lo]).astype(BF16)
        total[...] += dot_left(mixed, gprod)
        gmixed = dot_right(gprod, weight[...])
    part, prod, head = spread[:, :128], prods[:, :128], lead[...]
    gprod = (gmixed * part).astype(BF16)
    d_1[...] += dot_left((head * part).astype(BF16), gprod)
    gfirst = dot_right(gprod, w1[...])
    gspread[:, :128] = (gmixed * prod + gfirst * head).astype(BF16)
    glead[...] = pltpu.roll(gfirst * part, 96, 1)

    @pl.when(step == pl.num_programs(0) - 1)
    def _():
        grads[0:512, :] = d_out[...].astype(BF16)
        grads[512:768, :] = d_4[...].astype(BF16)
        grads[768:896, 0:256] = d_3[...].astype(BF16)
        grads[768:896, 256:384] = d_2[...].astype(BF16)
        grads[768:896, 384:512] = d_1[...].astype(BF16)


def down_kernel(active, middle, vecs, down_w, before, outputs):
    down = dot(active[...], down_w[...])
    outputs[...] = (middle[...] + vecs[SCALE_2 : SCALE_2 + 1, :] * down).astype(BF16)


def kernel_back_kernel(xwaves, gspread, tg, td, out, gs, gwaves, total):
    step = pl.program_id(0)

    @pl.when(step == 0)
    def _():
        total[...] = jnp.zeros_like(total)

    gs[...] = gspread[...].astype(F32)

    def block_of_lanes(block, carry):
        lanes = pl.ds(pl.multiple_of(LANES * block, LANES), LANES)
        square = jnp.concatenate(
            [
                jnp.concatenate(
                    [gs[r * 40 + OUT * col : r * 40 + OUT * col + OUT, lanes] for r in range(OUT)], axis=0
                ).astype(BF16)
                for col in range(TILES)
            ],
            axis=1,
        )
        gwaves[...] = dot(tg[...], square)
        for row in range(0, SLOTS, 16):
            here, there = slice(row, row + 16), slice(SLOTS + row, SLOTS + row + 16)
            sums = [total[pl.ds(SLOTS * k + row, 16), lanes] for k in range(4)]
            for col in range(TILES):
                at = slice(LANES * col, LANES * col + LANES)
                base = 2 * SLOTS * col + row
                real = xwaves[base : base + 16, lanes].astype(F32)
                imag = xwaves[base + SLOTS : base + SLOTS + 16, lanes].astype(F32)
                greal, gimag = gwaves[here, at], gwaves[there, at]
                sums = [
                    sums[0] + greal * real, sums[1] + gimag * imag, sums[2] + greal * imag, sums[3] + gimag * real
                ]
            for k in range(4):
                total[pl.ds(SLOTS * k + row, 16), lanes] = sums[k]
        return carry

    lax.fori_loop(0, 1024 // LANES, block_of_lanes, 0)

    @pl.when(step == pl.num_programs(0) - 1)
    def _():
        taps = jnp.dot(
            td[...], total[...], preferred_element_type=F32, precision=lax.Precision.HIGHEST
        )
        out[...] = jnp.concatenate([taps[:, :512], taps[:, 512:]], axis=0).astype(BF16)


def gates_back_kernel(gs_ext, glead, spec, tx, ty, gjoined, ext, waves, mixed_waves, ggates):
    step = pl.program_id(0)
    span = 48

    def widen(start, count):
        at = pl.ds(start, count)
        ext[at, :] = gs_ext[at, :].astype(F32)

    @pl.when(step == 0)
    def _():
        widen(0, 6 * span)

    widen(pl.multiple_of((OUT * step + 6) * span, 16), OUT * span)
    depthwise(ext, OUT * step, spec, tx, ty, waves, mixed_waves, ggates)
    gjoined[:, :128] = (ggates[:, :128] + glead[...]).astype(BF16)
    gjoined[:, 128:] = ggates[:, 128:].astype(BF16)


def in_back_kernel(
    gjoined, x_own, gmiddle, valid, vecs, in_w, mixer_grads, grad_kernel, ffn_sums, bias_sum,
    ginput, sent, kept,
    normed_all, gjoined_all, vec_sums,
):
    step = pl.program_id(0)
    chunk = x_own.shape[0]
    rows = pl.ds(pl.multiple_of(step * chunk, 16), chunk)

    @pl.when(step == 0)
    def _():
        vec_sums[...] = jnp.zeros_like(vec_sums)

    gjoined_all[rows, :] = gjoined[...]
    gnormed = dot_right(gjoined[...], in_w[...])
    normal, inverse = normalize(x_own[...].astype(F32))
    gain = vecs[GAIN_1 : GAIN_1 + 1, :]
    mask = valid[...]
    normed_all[rows, :] = ((normal * gain + vecs[SHIFT_1 : SHIFT_1 + 1, :]) * mask).astype(BF16)
    masked = gnormed * mask
    vec_sums[0:1, :] += jnp.sum(masked * normal, axis=0, keepdims=True)
    vec_sums[1:2, :] += jnp.sum(masked, axis=0, keepdims=True)
    ginput[...] = (gmiddle[...] + norm_back(masked, normal, inverse, gain)).astype(BF16)

    @pl.when(step == pl.num_programs(0) - 1)
    def _():
        def finish(for_in, for_others):
            for block in range(2):
                lanes = slice(512 * block, 512 * block + 512)
                for_in[lanes, :] = dot_left(normed_all[...], gjoined_all[:, lanes]).astype(BF16)
            for_others[0:896, :] = mixer_grads[...]
            for_others[896:1008, :] = grad_kernel[...]
            pieces = [vec_sums[0:2, :], ffn_sums[0:2, :]]
            pieces += [bias_sum[0:1, 512 * k : 512 * k + 512] for k in range(4)]
            pieces.append(jnp.zeros((8, 512), F32))
            for_others[1008:1024, :] = jnp.concatenate(pieces, axis=0).astype(BF16)

        even = lax.axis_index("col") % 2 == 0
        pl.when(even)(lambda: finish(kept, sent))
        pl.when(jnp.logical_not(even))(lambda: finish(sent, kept))


def expand_ffn_kernel(own, got, down_w, vecs, grad_down, grad_up, grad_scale):
    step = pl.program_id(0)

    @pl.when(step == 0)
    def _():
        grad_scale[...] = jnp.zeros_like(grad_scale)

    def expand(down, up):
        block = down[...].astype(F32).T
        grad_down[...] = block
        grad_up[...] = up[...].astype(F32)
        grad_scale[...] += jnp.sum(block * down_w[...].astype(F32), axis=0, keepdims=True)

    even = lax.axis_index("col") % 2 == 0
    pl.when(even)(lambda: expand(own, got))
    pl.when(jnp.logical_not(even))(lambda: expand(got, own))

    @pl.when(step == pl.num_programs(0) - 1)
    def _():
        grad_scale[...] = grad_scale[...] / vecs[SCALE_2 : SCALE_2 + 1, :]


def expand_rest_kernel(
    own, got, out_w, vecs, grad_in, grad_conv, grad_1, grad_2, grad_3, grad_4, grad_out,
    gain_1, shift_1, scale_1, gain_2, shift_2, grad_bias,
):
    def expand(first, other):
        grad_in[:, :512] = first[:512, :].astype(F32)
        grad_in[:, 512:] = first[512:, :].astype(F32)
        block = other[:512, :].astype(F32)
        grad_out[...] = block
        scaled = jnp.sum(block * out_w[...].astype(F32), axis=0, keepdims=True)
        scale_1[...] = scaled / vecs[SCALE_1 : SCALE_1 + 1, :]
        grad_4[...] = other[512:768, :].astype(F32)
        square = other[768:896, :].astype(F32)
        grad_3[...] = square[:, 0:256]
        grad_2[...] = square[64:128, 256:384]
        grad_1[...] = square[32:64, 384 + 64 : 512]
        tail = other[896:1024, :].astype(F32)
        taps = jnp.concatenate([tail[:56], tail[56:112]], axis=1)[:, 32:]
        for row in range(TAPS):
            grad_conv[row] = taps[TAPS * row : TAPS * row + TAPS]
        for row, ref in enumerate((gain_1, shift_1, gain_2, shift_2)):
            ref[...] = tail[112 + row : 113 + row]
        for k in range(4):
            grad_bias[:, 512 * k : 512 * k + 512] = tail[116 + k : 117 + k]

    even = lax.axis_index("col") % 2 == 0
    pl.when(even)(lambda: expand(own, got))
    pl.when(jnp.logical_not(even))(lambda: expand(got, own))


def whole(shape):
    return pl.BlockSpec(shape, lambda i: (0,) * len(shape), pipeline_mode=pl.Buffered(1))


def chunked(shape):
    return pl.BlockSpec(shape, lambda i: (i,) + (0,) * (len(shape) - 1))


def held(shape):
    return pl.BlockSpec(shape, lambda i: (0,) * len(shape))


def params(limit_mib):
    return pltpu.CompilerParams(vmem_limit_bytes=limit_mib * 1024 * 1024, dimension_semantics=("arbitrary",))


def cost(micros):
    return pl.CostEstimate(flops=int(micros * 1e10), bytes_accessed=int(micros * 3e7), transcendentals=0)


def shaped(shape, dtype):
    return jax.ShapeDtypeStruct(shape, dtype)


AXES = ("row", "col")


class Reducer:
    def __init__(self):
        self.rows = lax.axis_size("row")
        self.cols = lax.axis_size("col")
        self.row_at = lax.axis_index("row")
        self.col_at = lax.axis_index("col")
        bits = [("row", 1 << b) for b in range(self.rows.bit_length() - 1)]
        bits += [("col", 1 << b) for b in range(1, self.cols.bit_length() - 1)]
        self.steps = list(zip(bits, bits[1:-1] + [bits[0], bits[-1]]))
        self.core_step = (("col", 1), ("col", 1))
        self.core = self.col_at & 1

    def pairs(self, step):
        result = []
        for r in range(self.rows):
            for c in range(self.cols):
                axis, mask = step[c & 1]
                r2, c2 = (r ^ mask, c) if axis == "row" else (r, c ^ mask)
                result.append((r * self.cols + c, r2 * self.cols + c2))
        return result

    def bit(self, step):
        values = [((self.row_at if axis == "row" else self.col_at) & mask) != 0 for axis, mask in step]
        return jnp.where(self.core == 0, values[0], values[1]).astype(jnp.int32)

    def swap(self, block, step):
        return lax.ppermute(block, AXES, self.pairs(step))

    def open(self, sent, kept):
        return Sum(self, sent, kept)


class Sum:
    def __init__(self, reducer, sent, kept):
        self.reducer = reducer
        self.sent, self.kept, self.got = sent, kept, None
        count = len(reducer.steps)
        self.plan = [reducer.core_step] + reducer.steps + reducer.steps[-2::-1] + [reducer.core_step]
        self.halvings = count
        self.stage = 0

    @property
    def done(self):
        return self.stage == len(self.plan)

    def swap(self):
        self.got = self.reducer.swap(self.sent, self.plan[self.stage])

    def combine(self):
        sent, kept, got, stage = self.sent, self.kept, self.got, self.stage
        self.stage += 1
        self.got = None
        steps = self.reducer.steps
        if stage < self.halvings - 1:
            bit = self.reducer.bit(steps[stage])
            half = kept.shape[0] // 2

            def summed(at):
                pieces = [lax.dynamic_slice_in_dim(a, at * half, half, 0).astype(F32) for a in (kept, got)]
                return (pieces[0] + pieces[1]).astype(BF16)

            self.sent, self.kept = summed(1 - bit), summed(bit)
        elif stage <= self.halvings:
            self.sent = self.kept = (kept.astype(F32) + got.astype(F32)).astype(BF16)
        elif not self.done:
            bit = self.reducer.bit(self.plan[stage]) == 1
            self.sent = self.kept = jnp.concatenate([jnp.where(bit, got, kept), jnp.where(bit, kept, got)], axis=0)
        else:
            self.got = got

    def advance(self):
        self.swap()
        self.combine()


def shift_pairs(count):
    forward = [(i, i + 1) for i in range(count - 1)]
    return forward, [(b, a) for a, b in forward]


def on_device(
    activations, gain_first, shift_first, in_weight, conv_kernel, mix_first, mix_second, mix_third,
    mix_fourth, out_weight, scale_mixer, gain_second, shift_second, up_weight, up_bias, down_weight,
    scale_mlp, valid_pixels, tile_images, cotangent,
):
    tile_rows, tile_cols, width = activations.shape
    pixels = tile_rows * tile_cols
    hidden = up_weight.shape[1]
    gate_count = conv_kernel.shape[-1]
    joined_count = in_weight.shape[1]
    lead_count = joined_count - gate_count
    span = tile_cols + 8
    ext_rows = tile_rows + 2 * HALO
    ext_pixels = ext_rows * span
    tab = tables()
    down_pairs, up_pairs = shift_pairs(lax.axis_size("row"))
    right_pairs, left_pairs = shift_pairs(lax.axis_size("col"))

    row_at, col_at = lax.axis_index("row"), lax.axis_index("col")
    row_last, col_last = lax.axis_size("row") - 1, lax.axis_size("col") - 1
    own_image = tile_images[row_at, col_at]

    def same(row, col, inside):
        return jnp.logical_and(inside, tile_images[row, col] == own_image)

    same_up = same(jnp.maximum(row_at - 1, 0), col_at, row_at > 0)
    same_down = same(jnp.minimum(row_at + 1, row_last), col_at, row_at < row_last)
    same_left = same(row_at, jnp.maximum(col_at - 1, 0), col_at > 0)
    same_right = same(row_at, jnp.minimum(col_at + 1, col_last), col_at < col_last)

    def rows_around(block):
        return lax.ppermute(block[-HALO:], "row", down_pairs), lax.ppermute(block[:HALO], "row", up_pairs)

    def taller(above, block, below, outside):
        blank = jnp.asarray(outside, BF16)
        above, below = jnp.where(same_up, above, blank), jnp.where(same_down, below, blank)
        return jnp.concatenate([above, block, below], axis=0)

    def cols_around(from_left, from_right):
        return lax.ppermute(from_left, "col", right_pairs), lax.ppermute(from_right, "col", left_pairs)

    def wider(left, tall, right, outside):
        depth = tall.shape[-1]
        blank = jnp.asarray(outside, BF16)
        left, right = jnp.where(same_left, left, blank), jnp.where(same_right, right, blank)
        filler = jnp.full((ext_rows, span - tile_cols - 2 * HALO, depth), blank)
        return jnp.concatenate([left, tall, right, filler], axis=1).reshape(ext_pixels, depth)

    marked = jnp.where(valid_pixels[..., None] != 0, activations, jnp.asarray(OUTSIDE, BF16))
    above, below = rows_around(marked)
    tall = taller(above, marked, below, OUTSIDE)
    sides = tall[:, -HALO:], tall[:, :HALO]
    (sides, conv_kernel, mix_first, mix_second, valid_pixels) = lax.optimization_barrier(
        (sides, conv_kernel, mix_first, mix_second, valid_pixels)
    )
    left, right = cols_around(*sides)

    x_own = activations.reshape(pixels, width)
    cot = cotangent.reshape(pixels, width)
    valid = valid_pixels.astype(F32).reshape(pixels, 1)
    vecs = jnp.stack(
        [gain_first, shift_first, scale_mixer, gain_second, shift_second, scale_mlp, scale_mlp, scale_mlp]
    ).astype(F32)
    bias = up_bias.astype(F32).reshape(1, hidden)
    taps = jnp.pad(conv_kernel.astype(F32).reshape(TAPS * TAPS, gate_count), ((0, 0), (lead_count, 0)))
    spec = jnp.dot(tab["spectrum"], taps, precision=lax.Precision.HIGHEST, preferred_element_type=F32)
    w1 = jnp.zeros((128, 128), BF16).at[32:64, 64:128].set(mix_first)
    w2 = jnp.zeros((128, 128), BF16).at[64:128, :].set(mix_second)
    w3, w4 = mix_third, mix_fourth
    (left, right, spec, w1, w2, valid, vecs, bias) = lax.optimization_barrier(
        (left, right, spec, w1, w2, valid, vecs, bias)
    )
    x_ext = wider(left, tall, right, OUTSIDE)

    chunk = OUT * tile_cols
    steps = tile_rows // OUT
    (
        xwaves, spread, prods, lead, middle, active, slope, grad_down,
    ) = pl.pallas_call(
        forward_kernel,
        grid=(steps,),
        in_specs=[
            whole((ext_pixels, width)), chunked((chunk, width)), chunked((chunk, 1)),
            chunked((chunk, width)), whole((8, width)), whole((1, hidden)), whole((width, joined_count)),
            whole((128, 128)), whole((128, 128)), whole(w3.shape), whole(w4.shape), whole((width, width)),
            whole((width, hidden)), whole((3 * SLOTS, joined_count)), whole(tab["window"].shape),
            whole(tab["tile_back"].shape),
        ],
        out_specs=[
            chunked((2 * SLOTS * TILES, joined_count)), chunked((chunk, joined_count)),
            chunked((chunk, joined_count)), chunked((chunk, 128)), chunked((chunk, width)), chunked((chunk, hidden)),
            chunked((chunk, hidden)), held((hidden, width)),
        ],
        out_shape=[
            shaped((steps * 2 * SLOTS * TILES, joined_count), BF16), shaped((pixels, joined_count), F32),
            shaped((pixels, joined_count), F32), shaped((pixels, 128), F32),
            shaped((pixels, width), F32), shaped((pixels, hidden), BF16), shaped((pixels, hidden), BF16),
            shaped((hidden, width), BF16),
        ],
        scratch_shapes=[
            pltpu.VMEM((ext_pixels, joined_count + 128), F32),
            pltpu.VMEM((2 * SLOTS, LANES * TILES), F32), pltpu.VMEM((2 * SLOTS, LANES * TILES), BF16),
            pltpu.VMEM((pixels, hidden), BF16), pltpu.VMEM((pixels, width), BF16),
        ],
        compiler_params=params(58),
        cost_estimate=cost(40),
        name="forward",
    )(
        x_ext, x_own, valid, cot, vecs, bias, in_weight, w1, w2, w3, w4, out_weight, up_weight,
        spec, tab["window"], tab["tile_back"],
    )

    rows = 256
    count = pixels // rows
    gmiddle, ffn_sent, ffn_kept, ffn_sums, bias_sum = pl.pallas_call(
        ffn_back_kernel,
        grid=(count,),
        in_specs=[
            chunked((rows, width)), chunked((rows, hidden)), chunked((rows, width)), chunked((rows, 1)),
            whole((8, width)), whole((hidden, width)), whole((width, hidden)), whole((hidden, width)),
        ],
        out_specs=[
            chunked((rows, width)), held((hidden, width)), held((hidden, width)), held((8, width)),
            held((8, hidden)),
        ],
        out_shape=[
            shaped((pixels, width), F32), shaped((hidden, width), BF16), shaped((hidden, width), BF16),
            shaped((8, width), F32),
            shaped((8, hidden), F32),
        ],
        scratch_shapes=[pltpu.VMEM((pixels, width), BF16), pltpu.VMEM((pixels, hidden), BF16)],
        compiler_params=params(48),
        cost_estimate=cost(16),
        name="ffn_back",
    )(cot, slope, middle, valid, vecs, down_weight, up_weight, grad_down)

    reducer = Reducer()
    ffn = reducer.open(ffn_sent, ffn_kept)
    ffn.swap()

    gspread, glead, mixer_grads = pl.pallas_call(
        mixer_back_kernel,
        grid=(count,),
        in_specs=[
            chunked((rows, width)), chunked((rows, joined_count)), chunked((rows, joined_count)),
            chunked((rows, 128)), whole((8, width)), whole((128, 128)), whole((128, 128)), whole(w3.shape),
            whole(w4.shape), whole((width, width)),
        ],
        out_specs=[chunked((rows, joined_count)), chunked((rows, 128)), held((896, width))],
        out_shape=[
            shaped((pixels, joined_count), BF16), shaped((pixels, 128), F32), shaped((896, width), BF16),
        ],
        scratch_shapes=[
            pltpu.VMEM((width, width), F32), pltpu.VMEM(w4.shape, F32), pltpu.VMEM(w3.shape, F32),
            pltpu.VMEM((128, 128), F32), pltpu.VMEM((128, 128), F32),
        ],
        compiler_params=params(48),
        cost_estimate=cost(12),
        name="mixer_back",
    )(gmiddle, spread, prods, lead, vecs, w1, w2, w3, w4, out_weight)

    tie = lax.optimization_barrier
    (gspread, ffn.kept, ffn.got) = tie((gspread, ffn.kept, ffn.got))
    block = gspread.reshape(tile_rows, tile_cols, joined_count)
    above, below = rows_around(block)
    grad_kernel = pl.pallas_call(
        kernel_back_kernel,
        grid=(steps,),
        in_specs=[
            chunked((2 * SLOTS * TILES, joined_count)), chunked((chunk, joined_count)),
            whole(tab["tile"].shape), whole(tab["kernel_back"].shape),
        ],
        out_specs=held((112, width)),
        out_shape=shaped((112, width), BF16),
        scratch_shapes=[
            pltpu.VMEM((chunk, joined_count), F32), pltpu.VMEM((2 * SLOTS, LANES * TILES), F32),
            pltpu.VMEM((4 * SLOTS, joined_count), F32),
        ],
        compiler_params=params(48),
        cost_estimate=cost(9),
        name="kernel_back",
    )(xwaves, gspread, tab["tile"], tab["kernel_back"])
    (above, below, grad_kernel, ffn.kept) = tie((above, below, grad_kernel, ffn.kept))
    tall = taller(above, block, below, 0.0)
    sides = tall[:, -HALO:], tall[:, :HALO]
    (sides, ffn.kept) = tie((sides, ffn.kept))
    left, right = cols_around(*sides)
    ffn.combine()
    (left, right, ffn.sent, ffn.kept) = tie((left, right, ffn.sent, ffn.kept))
    ffn.swap()
    gs_ext = wider(left, tall, right, 0.0)

    gjoined = pl.pallas_call(
        gates_back_kernel,
        grid=(steps,),
        in_specs=[
            whole((ext_pixels, joined_count)), chunked((chunk, 128)),
            pl.BlockSpec((3 * SLOTS, joined_count), lambda i: (1, 0), pipeline_mode=pl.Buffered(1)),
            whole(tab["window"].shape), whole(tab["tile_back"].shape),
        ],
        out_specs=chunked((chunk, joined_count)),
        out_shape=shaped((pixels, joined_count), BF16),
        scratch_shapes=[
            pltpu.VMEM((ext_pixels, joined_count), F32), pltpu.VMEM((2 * SLOTS, LANES * TILES), F32),
            pltpu.VMEM((2 * SLOTS, LANES * TILES), BF16), pltpu.VMEM((chunk, joined_count), F32),
        ],
        compiler_params=params(48),
        cost_estimate=cost(11),
        name="gates_back",
    )(gs_ext, glead, spec, tab["window"], tab["tile_back"])
    (gjoined, ffn.got) = tie((gjoined, ffn.got))
    ffn.combine()
    (gjoined, ffn.sent, ffn.kept) = tie((gjoined, ffn.sent, ffn.kept))
    ffn.swap()

    ginput, rest_sent, rest_kept = pl.pallas_call(
        in_back_kernel,
        grid=(count,),
        in_specs=[
            chunked((rows, joined_count)), chunked((rows, width)), chunked((rows, width)), chunked((rows, 1)),
            whole((8, width)), whole((width, joined_count)), whole((896, width)), whole((112, width)),
            whole((8, width)), whole((8, hidden)),
        ],
        out_specs=[chunked((rows, width)), held((joined_count, width)), held((joined_count, width))],
        out_shape=[
            shaped((pixels, width), BF16), shaped((joined_count, width), BF16), shaped((joined_count, width), BF16),
        ],
        scratch_shapes=[
            pltpu.VMEM((pixels, width), BF16), pltpu.VMEM((pixels, joined_count), BF16), pltpu.VMEM((8, width), F32),
        ],
        compiler_params=params(48),
        cost_estimate=cost(8),
        name="in_back",
    )(
        gjoined, x_own, gmiddle, valid, vecs, in_weight, mixer_grads, grad_kernel, ffn_sums, bias_sum,
    )
    rest = reducer.open(rest_sent, rest_kept)
    rest.swap()
    (rest.kept, ffn.got) = tie((rest.kept, ffn.got))
    ffn.combine()
    ffn.swap()

    def down(active, before, first, blocks):
        return pl.pallas_call(
            down_kernel,
            grid=(blocks,),
            in_specs=[
                pl.BlockSpec((rows, hidden), lambda i: (i + first, 0)),
                pl.BlockSpec((rows, width), lambda i: (i + first, 0)), whole((8, width)), whole((hidden, width)),
                pl.BlockSpec(memory_space=pl.ANY),
            ],
            out_specs=pl.BlockSpec((rows, width), lambda i: (i + first, 0)),
            out_shape=shaped((pixels, width), BF16),
            input_output_aliases={4: 0} if first else {},
            compiler_params=params(48),
            cost_estimate=cost(4),
            name="down",
        )(active, middle, vecs, down_weight, before)

    (active, rest.sent, ffn.sent) = tie((active, rest.sent, ffn.sent))
    outputs = down(active, jnp.zeros((8, 128), BF16), 0, count // 2)

    def onward(way, *others):
        values = tie((way.kept, way.got) + others)
        way.kept, way.got = values[:2]
        way.combine()
        if not way.done:
            way.swap()
        return values[2:]

    (outputs,) = onward(rest, outputs)
    (rest.kept,) = onward(ffn, rest.kept)
    (outputs, rest.sent, ffn.sent) = tie((outputs, rest.sent, ffn.sent))
    outputs = down(active, outputs, count // 2, count - count // 2)
    (outputs,) = onward(rest, outputs)
    expand_ffn = pl.pallas_call(
        expand_ffn_kernel,
        grid=(hidden // width,),
        in_specs=[
            chunked((width, width)), chunked((width, width)), chunked((width, width)), whole((8, width)),
        ],
        out_specs=[
            chunked((width, width)), pl.BlockSpec((width, width), lambda i: (0, i)), held((1, width)),
        ],
        out_shape=[shaped((hidden, width), F32), shaped((width, hidden), F32), shaped((1, width), F32)],
        compiler_params=params(32),
        cost_estimate=cost(5),
        name="expand_ffn",
    )
    expanded = None
    for who in "frfrfrrfrfr":
        way, other = (ffn, rest) if who == "f" else (rest, ffn)
        if not way.done:
            (other.kept,) = onward(way, other.kept)
        if ffn.done and expanded is None:
            expanded = expand_ffn(ffn.kept, ffn.got, down_weight, vecs)
            (rest.kept, expanded) = tie((rest.kept, expanded))
    while not (ffn.done and rest.done):
        for way in (ffn, rest):
            if not way.done:
                onward(way)
    if expanded is None:
        expanded = expand_ffn(ffn.kept, ffn.got, down_weight, vecs)
    grad_down_weight, grad_up_weight, scale_2 = expanded
    rest_own, rest_got = rest.kept, rest.got
    vector = shaped((1, width), F32)
    whole_block = pl.BlockSpec(memory_space=pltpu.VMEM)
    (
        grad_in_weight, grad_conv, grad_1, grad_2, grad_3, grad_4, grad_out,
        gain_1, shift_1, scale_1, gain_2, shift_2, grad_bias,
    ) = pl.pallas_call(
        expand_rest_kernel,
        in_specs=[whole_block] * 4,
        out_specs=[whole_block] * 13,
        out_shape=[
            shaped(in_weight.shape, F32), shaped(conv_kernel.shape, F32), shaped(mix_first.shape, F32),
            shaped(mix_second.shape, F32), shaped(w3.shape, F32), shaped(w4.shape, F32), shaped((width, width), F32),
            vector, vector, vector, vector, vector, shaped((1, hidden), F32),
        ],
        compiler_params=pltpu.CompilerParams(vmem_limit_bytes=32 * 1024 * 1024),
        cost_estimate=cost(5),
        name="expand_rest",
    )(rest_own, rest_got, out_weight, vecs)
    return (
        outputs.reshape(activations.shape),
        ginput.reshape(activations.shape),
        gain_1.reshape(width),
        shift_1.reshape(width),
        grad_in_weight,
        grad_conv,
        grad_1,
        grad_2,
        grad_3,
        grad_4,
        grad_out,
        scale_1.reshape(width),
        gain_2.reshape(width),
        shift_2.reshape(width),
        grad_up_weight,
        grad_bias.reshape(hidden),
        grad_down_weight,
        scale_2.reshape(width),
    )


def solution(mesh):
    tiles = P("row", "col", None)
    in_specs = (tiles,) + (P(),) * 16 + (P("row", "col"), P(), tiles)
    out_specs = (tiles, tiles) + (P(),) * 16
    return jax.shard_map(on_device, mesh=mesh, in_specs=in_specs, out_specs=out_specs, check_vma=False)
```

```python
import math
from functools import partial

import jax
import jax.numpy as jnp
import ml_dtypes
import numpy as np
from jax import lax
from jax.experimental import pallas as pl
from jax.experimental.pallas import tpu as pltpu
from jax.sharding import PartitionSpec as P

EPS = 1e-06
TAPS = 7
HALO = 3
OUT = 8
WIN = OUT + TAPS - 1
PITCH = 16
SLOTS = 112
OUTSIDE = 64.0
COS_SCALE = 1.422015
SIN_SCALE = 1.818765
TILES = 5
LANES = 512
BF16 = jnp.bfloat16
F32 = jnp.float32


def frequencies():
    pairs, own, seen = [], [], set()
    for u in range(WIN):
        for v in range(WIN):
            if (u, v) in seen:
                continue
            twin = ((-u) % WIN, (-v) % WIN)
            seen.update([(u, v), twin])
            (own if twin == (u, v) else pairs).append((u, v))
    return np.array(pairs + own), np.array([2.0] * len(pairs) + [1.0] * len(own))


def angles(rows, cols, pitch):
    freq, _ = frequencies()
    a = np.arange(rows)[:, None]
    b = np.arange(pitch)[None, :]
    theta = 2 * np.pi * (freq[:, 0, None, None] * a + freq[:, 1, None, None] * b) / WIN
    live = np.broadcast_to(b < cols, (rows, pitch))
    cos = np.zeros((SLOTS, rows * pitch))
    sin = np.zeros((SLOTS, rows * pitch))
    cos[: len(freq)] = (np.cos(theta) * live).reshape(len(freq), -1)
    sin[: len(freq)] = (np.sin(theta) * live).reshape(len(freq), -1)
    return cos, sin


def tables():
    _, weight = frequencies()
    weight = np.concatenate([weight, np.zeros(SLOTS - len(weight))])[:, None]
    area = WIN * WIN

    def ahead(cos, sin):
        return np.concatenate([COS_SCALE * cos, -SIN_SCALE * sin])

    def back(cos, sin):
        return np.concatenate([weight * COS_SCALE * cos, -weight * SIN_SCALE * sin]).T

    window = angles(WIN, WIN, PITCH)
    tile = angles(OUT, OUT, OUT)
    cos, sin = angles(TAPS, TAPS, TAPS)
    third = 1.0 / 3.0
    spectrum = np.concatenate(
        [
            cos * (third / (area * COS_SCALE**2)),
            -sin * (third / (area * COS_SCALE * SIN_SCALE)),
            cos * (third / (area * SIN_SCALE**2)),
        ]
    )
    wide = weight * third / area
    kernel_back = np.concatenate(
        [
            wide * cos / COS_SCALE**2,
            wide * cos / SIN_SCALE**2,
            -wide * sin / (COS_SCALE * SIN_SCALE),
            wide * sin / (COS_SCALE * SIN_SCALE),
        ]
    ).T
    kernel_back = np.concatenate([kernel_back, np.zeros((7, 4 * SLOTS))])
    half = ml_dtypes.bfloat16
    return dict(
        window=ahead(*window).astype(half),
        tile=ahead(*tile).astype(half),
        window_back=back(*window).astype(half),
        tile_back=back(*tile).astype(half),
        spectrum=np.concatenate([spectrum, spectrum[:, ::-1]]).astype(np.float32),
        kernel_back=kernel_back.astype(np.float32),
    )


def dot(left, right):
    return jnp.dot(left, right, preferred_element_type=F32)


def dot_right(left, right):
    return lax.dot_general(left, right, (((1,), (1,)), ((), ())), preferred_element_type=F32)


def dot_left(left, right):
    return lax.dot_general(left, right, (((0,), (0,)), ((), ())), preferred_element_type=F32)


def normalize(values):
    center = values - jnp.mean(values, axis=-1, keepdims=True)
    inverse = lax.rsqrt(jnp.mean(center * center, axis=-1, keepdims=True) + EPS)
    return center * inverse, inverse


def norm_back(masked, normal, inverse, gain):
    scaled = masked * gain
    centered = scaled - jnp.mean(scaled, axis=-1, keepdims=True)
    return inverse * (centered - normal * jnp.mean(scaled * normal, axis=-1, keepdims=True))


def gelu_pair(x):
    cumulative = 0.5 + 0.5 * lax.erf(x * math.sqrt(0.5))
    density = jnp.exp(-0.5 * x * x) * (1.0 / math.sqrt(2.0 * math.pi))
    return x * cumulative, cumulative + x * density


UP, DOWN, LEFT, RIGHT = range(4)


def fill(source, near, outside, above, own, below):
    edge, body = above.shape[0], own.shape[0]
    source[0:edge, :] = jnp.where(near[UP] != 0, above[...].astype(F32), outside)
    source[edge : edge + body, :] = own[...].astype(F32)
    source[edge + body : 2 * edge + body, :] = jnp.where(near[DOWN] != 0, below[...].astype(F32), outside)


def widen(ext, lanes, near, outside, source, left, right, first_row, rows):
    for r in range(rows):
        row = first_row + r
        line = source[pl.ds(pl.multiple_of(row * 40, 8), 40), :]
        depth = line.shape[1]
        before = jnp.where(near[LEFT] != 0, left[row].astype(F32), outside)
        after = jnp.where(near[RIGHT] != 0, right[row].astype(F32), outside)
        pieces = [before, line, after, jnp.full((2, depth), outside, F32)]
        ext[pl.ds(pl.multiple_of(row * 48, 8), 48), lanes] = jnp.concatenate(pieces, axis=0)


def depthwise(ext, first_row, spec, tx, ty, waves, mixed_waves, result_ref, kept=None):
    span = 48

    def block_of_lanes(block, carry):
        lanes = pl.ds(pl.multiple_of(LANES * block, LANES), LANES)
        window = jnp.concatenate(
            [
                jnp.concatenate(
                    [
                        ext[pl.ds(pl.multiple_of((first_row + r) * span + OUT * col, 8), PITCH), lanes]
                        for r in range(WIN)
                    ],
                    axis=0,
                ).astype(BF16)
                for col in range(TILES)
            ],
            axis=1,
        )
        waves[...] = dot(tx[...], window)
        for row in range(0, SLOTS, 16):
            here, there = slice(row, row + 16), slice(SLOTS + row, SLOTS + row + 16)
            low, cross, high = (spec[pl.ds(SLOTS * k + row, 16), lanes] for k in range(3))
            for col in range(TILES):
                at = slice(LANES * col, LANES * col + LANES)
                real, imag = waves[here, at], waves[there, at]
                mixed_waves[here, at] = (low * real + cross * imag).astype(BF16)
                mixed_waves[there, at] = (high * imag - cross * real).astype(BF16)
                if kept is not None:
                    base = 2 * SLOTS * col + row
                    kept[base : base + 16, lanes] = real.astype(BF16)
                    kept[base + SLOTS : base + SLOTS + 16, lanes] = imag.astype(BF16)
        result = dot(ty[...], mixed_waves[...])
        for col in range(TILES):
            for r in range(OUT):
                result_ref[r * 40 + OUT * col : r * 40 + OUT * col + OUT, lanes] = result[
                    OUT * r : OUT * r + OUT, LANES * col : LANES * col + LANES
                ]
        return carry

    lax.fori_loop(0, 1024 // LANES, block_of_lanes, 0)


GAIN_1, SHIFT_1, SCALE_1, GAIN_2, SHIFT_2, SCALE_2 = range(6)


def copies(pairs, sems):
    return [pltpu.make_async_copy(src, dst, sems.at[k]) for k, (src, dst) in enumerate(pairs)]


class Sender:
    def __init__(self, hbm, slots, sems, step):
        self.hbm, self.slots, self.sems, self.step = hbm, slots, sems, step
        self.rows = slots.shape[1]
        self.slot = lax.rem(step, 2)
        self.ref = slots.at[self.slot]

    def copy(self, step, slot):
        at = pl.ds(pl.multiple_of(step * self.rows, 16), self.rows)
        return pltpu.make_async_copy(self.slots.at[slot], self.hbm.at[at, :], self.sems.at[slot])

    def free(self):
        pl.when(self.step >= 2)(lambda: self.copy(self.step - 2, self.slot).wait())

    def start(self):
        self.copy(self.step, self.slot).start()

    def finish(self):
        self.copy(self.step - 1, 1 - self.slot).wait()
        self.copy(self.step, self.slot).wait()


def forward_kernel(
    near, x_own, valid, cot, vecs, up_bias, w1, w2, w3, tx, ty,
    x_above, x_marked, x_below, x_left, x_right, in_hbm, spec_hbm, w4_hbm, out_hbm, up_hbm,
    waves_hbm, spread_hbm, prods_hbm, lead_out, middle_out, active_hbm, slope_hbm, down_hbm,
    ext, waves, mixed_waves, active_all, gdown_all,
    x_source, x_ext, in_w, spec, w4, out_w, up_w, waves_slots, spread_slots, prods_slots, slope_slots, grad_down,
    in_sems, waves_sems, spread_sems, prods_sems, slope_sems, active_sems, down_sems,
):
    step = pl.program_id(0)
    last = pl.num_programs(0) - 1
    span = 48
    chunk = lead_out.shape[0]
    gain = vecs[GAIN_1 : GAIN_1 + 1, :]
    shift = vecs[SHIFT_1 : SHIFT_1 + 1, :]
    loads = copies(
        [(in_hbm, in_w), (spec_hbm.at[: 3 * SLOTS, :], spec), (w4_hbm, w4), (out_hbm, out_w), (up_hbm, up_w)],
        in_sems,
    )

    def begin():
        for load in loads:
            load.start()

    pl.when(step == 0)(begin)

    def arrived(*which):
        def wait():
            for k in which:
                loads[k].wait()

        pl.when(step == 0)(wait)

    waves_to = Sender(waves_hbm, waves_slots, waves_sems, step)
    spread_to = Sender(spread_hbm, spread_slots, spread_sems, step)
    prods_to = Sender(prods_hbm, prods_slots, prods_sems, step)
    slope_to = Sender(slope_hbm, slope_slots, slope_sems, step)
    spread, prods = spread_to.ref, prods_to.ref

    def project(start, rows):
        at = pl.ds(start, rows)
        values = x_ext[at, :]
        normal, _ = normalize(values)
        normed = jnp.where(values[:, :1] < 0.5 * OUTSIDE, normal * gain + shift, 0.0).astype(BF16)
        for block in range(2):
            lanes = slice(512 * block, 512 * block + 512)
            joined = dot(normed, in_w[:, lanes])
            if block == 0:
                ext[at, 1024:1152] = joined[:, :128]
            low = joined.astype(BF16)
            ext[at, lanes] = low.astype(F32)

    arrived(0)

    @pl.when(step == 0)
    def _():
        fill(x_source, near, OUTSIDE, x_above, x_marked, x_below)
        widen(x_ext, slice(0, 512), near, OUTSIDE, x_source, x_left, x_right, 0, 6)
        project(0, 6 * span)

    widen(x_ext, slice(0, 512), near, OUTSIDE, x_source, x_left, x_right, OUT * step + 6, OUT)

    project(pl.multiple_of((OUT * step + 6) * span, 16), OUT * span)

    arrived(1)
    waves_to.free()
    spread_to.free()
    depthwise(ext, OUT * step, spec, tx, ty, waves, mixed_waves, spread, waves_to.ref)
    waves_to.start()
    spread_to.start()

    lead = jnp.concatenate(
        [
            ext[pl.ds(pl.multiple_of((OUT * step + HALO + r) * span, 8), span), 1024:1152][HALO : HALO + 40]
            for r in range(OUT)
        ],
        axis=0,
    )
    lead = pltpu.roll(lead, 32, 1)
    lead_out[...] = lead
    mixed = lead * spread[:, :128]
    arrived(2, 3)
    prods_to.free()
    for weight, lo, hi in ((w1, 0, 128), (w2, 128, 256), (w3, 256, 512), (w4, 512, 1024)):
        produced = dot(mixed.astype(BF16), weight[...])
        prods[:, lo:hi] = produced
        mixed = produced * spread[:, lo:hi]
    prods_to.start()
    branch = dot(mixed.astype(BF16), out_w[...])
    middle = x_own[...].astype(F32) + vecs[SCALE_1 : SCALE_1 + 1, :] * branch
    middle_out[...] = middle
    normal, _ = normalize(middle)
    normed = (
        (normal * vecs[GAIN_2 : GAIN_2 + 1, :] + vecs[SHIFT_2 : SHIFT_2 + 1, :]) * valid[...]
    ).astype(BF16)
    rows = pl.ds(pl.multiple_of(step * chunk, 16), chunk)
    arrived(4)
    slope_to.free()
    for block in range(4):
        lanes = slice(512 * block, 512 * block + 512)
        pre = dot(normed, up_w[:, lanes]) + up_bias[:, lanes]
        active, slope = gelu_pair(pre)
        active_all[rows, lanes] = active.astype(BF16)
        slope_to.ref[:, lanes] = slope.astype(BF16)
    slope_to.start()
    gdown_all[rows, :] = (cot[...].astype(F32) * vecs[SCALE_2 : SCALE_2 + 1, :]).astype(BF16)

    def active_copy(number):
        at = pl.ds(pl.multiple_of(number * chunk, 16), chunk)
        return pltpu.make_async_copy(active_all.at[at, :], active_hbm.at[at, :], active_sems.at[number])

    active_copy(step).start()

    @pl.when(step == last)
    def _():
        parts = []
        for block in range(4):
            lanes = slice(512 * block, 512 * block + 512)
            grad_down[lanes, :] = dot_left(gdown_all[...], active_all[:, lanes]).astype(BF16)
            parts.append(
                pltpu.make_async_copy(grad_down.at[lanes, :], down_hbm.at[lanes, :], down_sems.at[block])
            )
            parts[-1].start()
        for sender in (waves_to, spread_to, prods_to, slope_to):
            sender.finish()
        for number in range(active_sems.shape[0]):
            active_copy(number).wait()
        for part in parts:
            part.wait()


def ffn_back_kernel(
    cot, slope, middle, valid, vecs, down_w, up_w, grad_down,
    gmiddle, sent, kept, vec_sums, bias_sum,
    normed_all, gpre_all,
):
    step = pl.program_id(0)
    chunk = cot.shape[0]
    rows = pl.ds(pl.multiple_of(step * chunk, 16), chunk)

    @pl.when(step == 0)
    def _():
        vec_sums[...] = jnp.zeros_like(vec_sums)
        bias_sum[...] = jnp.zeros_like(bias_sum)

    grad = cot[...].astype(F32)
    gdown = (grad * vecs[SCALE_2 : SCALE_2 + 1, :]).astype(BF16)
    gnormed = jnp.zeros((chunk, 512), F32)
    for block in range(4):
        lanes = slice(512 * block, 512 * block + 512)
        gactive = dot_right(gdown, down_w[lanes, :])
        gpre = (gactive * slope[:, lanes].astype(F32)).astype(BF16)
        gpre_all[rows, lanes] = gpre
        bias_sum[0:1, lanes] += jnp.sum(gpre.astype(F32), axis=0, keepdims=True)
        gnormed = gnormed + dot_right(gpre, up_w[:, lanes])
    normal, inverse = normalize(middle[...])
    gain = vecs[GAIN_2 : GAIN_2 + 1, :]
    mask = valid[...]
    normed_all[rows, :] = ((normal * gain + vecs[SHIFT_2 : SHIFT_2 + 1, :]) * mask).astype(BF16)
    masked = gnormed * mask
    vec_sums[0:1, :] += jnp.sum(masked * normal, axis=0, keepdims=True)
    vec_sums[1:2, :] += jnp.sum(masked, axis=0, keepdims=True)
    gmiddle[...] = grad + norm_back(masked, normal, inverse, gain)

    @pl.when(step == pl.num_programs(0) - 1)
    def _():
        def finish(for_up, for_down):
            for block in range(4):
                lanes = slice(512 * block, 512 * block + 512)
                for_up[lanes, :] = dot_left(normed_all[...], gpre_all[:, lanes]).astype(BF16)
            for_down[: grad_down.shape[0], :] = grad_down[...]

        even = lax.axis_index("col") % 2 == 0
        pl.when(even)(lambda: finish(sent, kept))
        pl.when(jnp.logical_not(even))(lambda: finish(kept, sent))


def mixer_back_kernel(
    gmiddle, spread, prods, lead, vecs, w1, w2, w3, w4, out_w, sent_before, kept_before,
    gspread, glead, sent, kept,
    d_out, d_4, d_3, d_2, d_1, grads, sems,
):
    step = pl.program_id(0)

    @pl.when(step == 0)
    def _():
        for total in (d_out, d_4, d_3, d_2, d_1):
            total[...] = jnp.zeros_like(total)

    grad = gmiddle[...]
    glow = (grad * vecs[SCALE_1 : SCALE_1 + 1, :]).astype(BF16)
    part, prod = spread[:, 512:1024], prods[:, 512:1024]
    d_out[...] += dot_left((prod * part).astype(BF16), glow)
    gmixed = dot_right(glow, out_w[...])
    for weight, total, lo, hi, below in (
        (w4, d_4, 512, 1024, 256), (w3, d_3, 256, 512, 128), (w2, d_2, 128, 256, 0)
    ):
        gspread[:, lo:hi] = (gmixed * prods[:, lo:hi]).astype(BF16)
        gprod = (gmixed * spread[:, lo:hi]).astype(BF16)
        mixed = (prods[:, below:lo] * spread[:, below:lo]).astype(BF16)
        total[...] += dot_left(mixed, gprod)
        gmixed = dot_right(gprod, weight[...])
    part, prod, head = spread[:, :128], prods[:, :128], lead[...]
    gprod = (gmixed * part).astype(BF16)
    d_1[...] += dot_left((head * part).astype(BF16), gprod)
    gfirst = dot_right(gprod, w1[...])
    gspread[:, :128] = (gmixed * prod + gfirst * head).astype(BF16)
    glead[...] = pltpu.roll(gfirst * part, 96, 1)

    @pl.when(step == pl.num_programs(0) - 1)
    def _():
        grads[0:448, :] = d_out[0:448, :].astype(BF16)
        grads[448:512, :] = jnp.zeros((64, 512), BF16)
        grads[512:576, :] = d_out[448:512, :].astype(BF16)
        grads[576:832, :] = d_4[...].astype(BF16)
        grads[832:960, 0:256] = d_3[...].astype(BF16)
        grads[832:960, 256:384] = d_2[...].astype(BF16)
        grads[832:960, 384:512] = d_1[...].astype(BF16)
        grads[960:1024, :] = jnp.zeros((64, 512), BF16)
        start = sent.shape[0] - 512

        def finish(first, second):
            parts = copies(
                [
                    (grads.at[0:512, :], first.at[start : start + 512, :]),
                    (grads.at[512:1024, :], second.at[start : start + 512, :]),
                ],
                sems,
            )
            for part in parts:
                part.start()
            for part in parts:
                part.wait()

        even = lax.axis_index("col") % 2 == 0
        pl.when(even)(lambda: finish(kept, sent))
        pl.when(jnp.logical_not(even))(lambda: finish(sent, kept))


def down_kernel(active, middle, vecs, down_w, before, outputs):
    down = dot(active[...], down_w[...])
    outputs[...] = (middle[...] + vecs[SCALE_2 : SCALE_2 + 1, :] * down).astype(BF16)


def kernel_back_kernel(xwaves, gspread, tg, td, out, gs, gwaves, total):
    step = pl.program_id(0)

    @pl.when(step == 0)
    def _():
        total[...] = jnp.zeros_like(total)

    gs[...] = gspread[...].astype(F32)

    def block_of_lanes(block, carry):
        lanes = pl.ds(pl.multiple_of(LANES * block, LANES), LANES)
        square = jnp.concatenate(
            [
                jnp.concatenate(
                    [gs[r * 40 + OUT * col : r * 40 + OUT * col + OUT, lanes] for r in range(OUT)], axis=0
                ).astype(BF16)
                for col in range(TILES)
            ],
            axis=1,
        )
        gwaves[...] = dot(tg[...], square)
        for row in range(0, SLOTS, 16):
            here, there = slice(row, row + 16), slice(SLOTS + row, SLOTS + row + 16)
            sums = [total[pl.ds(SLOTS * k + row, 16), lanes] for k in range(4)]
            for col in range(TILES):
                at = slice(LANES * col, LANES * col + LANES)
                base = 2 * SLOTS * col + row
                real = xwaves[base : base + 16, lanes].astype(F32)
                imag = xwaves[base + SLOTS : base + SLOTS + 16, lanes].astype(F32)
                greal, gimag = gwaves[here, at], gwaves[there, at]
                sums = [
                    sums[0] + greal * real, sums[1] + gimag * imag, sums[2] + greal * imag, sums[3] + gimag * real
                ]
            for k in range(4):
                total[pl.ds(SLOTS * k + row, 16), lanes] = sums[k]
        return carry

    lax.fori_loop(0, 1024 // LANES, block_of_lanes, 0)

    @pl.when(step == pl.num_programs(0) - 1)
    def _():
        taps = jnp.dot(
            td[...], total[...], preferred_element_type=F32, precision=lax.Precision.HIGHEST
        )
        out[...] = jnp.concatenate([taps[:, :512], taps[:, 512:]], axis=0).astype(BF16)


def gates_back_kernel(
    near, above, own, below, left, right, glead, spec, tx, ty, gjoined, source, ext, waves, mixed_waves, ggates
):
    step = pl.program_id(0)

    @pl.when(step == 0)
    def _():
        fill(source, near, 0.0, above, own, below)
        widen(ext, slice(0, 1024), near, 0.0, source, left, right, 0, 6)

    widen(ext, slice(0, 1024), near, 0.0, source, left, right, OUT * step + 6, OUT)
    depthwise(ext, OUT * step, spec, tx, ty, waves, mixed_waves, ggates)
    gjoined[:, :128] = (ggates[:, :128] + glead[...]).astype(BF16)
    gjoined[:, 128:] = ggates[:, 128:].astype(BF16)


def in_back_kernel(
    gjoined, x_own, gmiddle, valid, vecs, in_w, grad_kernel, ffn_sums, bias_sum,
    ginput, sent, kept,
    normed_all, gjoined_all, vec_sums,
):
    step = pl.program_id(0)
    chunk = x_own.shape[0]
    rows = pl.ds(pl.multiple_of(step * chunk, 16), chunk)

    @pl.when(step == 0)
    def _():
        vec_sums[...] = jnp.zeros_like(vec_sums)

    gjoined_all[rows, :] = gjoined[...]
    gnormed = dot_right(gjoined[...], in_w[...])
    normal, inverse = normalize(x_own[...].astype(F32))
    gain = vecs[GAIN_1 : GAIN_1 + 1, :]
    mask = valid[...]
    normed_all[rows, :] = ((normal * gain + vecs[SHIFT_1 : SHIFT_1 + 1, :]) * mask).astype(BF16)
    masked = gnormed * mask
    vec_sums[0:1, :] += jnp.sum(masked * normal, axis=0, keepdims=True)
    vec_sums[1:2, :] += jnp.sum(masked, axis=0, keepdims=True)
    ginput[...] = (gmiddle[...] + norm_back(masked, normal, inverse, gain)).astype(BF16)

    @pl.when(step == pl.num_programs(0) - 1)
    def _():
        def finish(first, second):
            first[0:512, :] = dot_left(normed_all[...], gjoined_all[:, 0:512]).astype(BF16)
            block = dot_left(normed_all[...], gjoined_all[:, 512:1024]).astype(BF16)
            first[512:576, :] = block[0:64, :]
            second[0:448, :] = block[64:512, :]
            second[448:560, :] = grad_kernel[...]
            pieces = [vec_sums[0:2, :], ffn_sums[0:2, :]]
            pieces += [bias_sum[0:1, 512 * k : 512 * k + 512] for k in range(4)]
            pieces.append(jnp.zeros((8, 512), F32))
            second[560:576, :] = jnp.concatenate(pieces, axis=0).astype(BF16)

        even = lax.axis_index("col") % 2 == 0
        pl.when(even)(lambda: finish(kept, sent))
        pl.when(jnp.logical_not(even))(lambda: finish(sent, kept))


def expand_early_kernel(
    own, got, down_w, out_w, vecs,
    grad_down, grad_up, scale_2, grad_out, grad_4, grad_3, grad_2, grad_1, scale_1,
):
    step = pl.program_id(0)

    @pl.when(step == 0)
    def _():
        scale_2[...] = jnp.zeros_like(scale_2)

    def expand(first, second):
        @pl.when(step < 4)
        def _():
            block = first[...].astype(F32).T
            grad_down[...] = block
            grad_up[...] = second[...].astype(F32)
            scale_2[...] += jnp.sum(block * down_w[...].astype(F32), axis=0, keepdims=True)

        @pl.when(step == 4)
        def _():
            scale_2[...] = scale_2[...] / vecs[SCALE_2 : SCALE_2 + 1, :]
            grad_out[0:448, :] = first[0:448, :].astype(F32)
            grad_out[448:512, :] = second[0:64, :].astype(F32)
            grad_4[...] = second[64:320, :].astype(F32)
            square = second[320:448, :].astype(F32)
            grad_3[...] = square[:, 0:256]
            grad_2[...] = square[64:128, 256:384]
            grad_1[...] = square[32:64, 384 + 64 : 512]
            summed = jnp.sum(grad_out[...] * out_w[...].astype(F32), axis=0, keepdims=True)
            scale_1[...] = summed / vecs[SCALE_1 : SCALE_1 + 1, :]

    even = lax.axis_index("col") % 2 == 0
    pl.when(even)(lambda: expand(own, got))
    pl.when(jnp.logical_not(even))(lambda: expand(got, own))


def expand_late_kernel(own, got, grad_in, grad_conv, gain_1, shift_1, gain_2, shift_2, grad_bias):
    def expand(first, second):
        grad_in[:, :512] = first[:512, :].astype(F32)
        grad_in[0:64, 512:] = first[512:576, :].astype(F32)
        grad_in[64:512, 512:] = second[0:448, :].astype(F32)
        tail = second[448:576, :].astype(F32)
        taps = jnp.concatenate([tail[:56], tail[56:112]], axis=1)[:, 32:]
        for row in range(TAPS):
            grad_conv[row] = taps[TAPS * row : TAPS * row + TAPS]
        for row, ref in enumerate((gain_1, shift_1, gain_2, shift_2)):
            ref[...] = tail[112 + row : 113 + row]
        for k in range(4):
            grad_bias[:, 512 * k : 512 * k + 512] = tail[116 + k : 117 + k]

    even = lax.axis_index("col") % 2 == 0
    pl.when(even)(lambda: expand(own, got))
    pl.when(jnp.logical_not(even))(lambda: expand(got, own))


def whole(shape):
    return pl.BlockSpec(shape, lambda i: (0,) * len(shape), pipeline_mode=pl.Buffered(1))


def chunked(shape):
    return pl.BlockSpec(shape, lambda i: (i,) + (0,) * (len(shape) - 1))


def held(shape):
    return pl.BlockSpec(shape, lambda i: (0,) * len(shape))


def params(limit_mib):
    return pltpu.CompilerParams(vmem_limit_bytes=limit_mib * 1024 * 1024, dimension_semantics=("arbitrary",))


def cost(micros):
    return pl.CostEstimate(flops=int(micros * 1e10), bytes_accessed=int(micros * 3e7), transcendentals=0)


def shaped(shape, dtype):
    return jax.ShapeDtypeStruct(shape, dtype)


AXES = ("row", "col")


class Reducer:
    def __init__(self):
        self.rows = lax.axis_size("row")
        self.cols = lax.axis_size("col")
        self.row_at = lax.axis_index("row")
        self.col_at = lax.axis_index("col")
        bits = [("row", 1 << b) for b in range(self.rows.bit_length() - 1)]
        bits += [("col", 1 << b) for b in range(1, self.cols.bit_length() - 1)]
        self.steps = list(zip(bits, bits[1:-1] + [bits[0], bits[-1]]))
        self.core_step = (("col", 1), ("col", 1))
        self.core = self.col_at & 1

    def pairs(self, step):
        result = []
        for r in range(self.rows):
            for c in range(self.cols):
                axis, mask = step[c & 1]
                r2, c2 = (r ^ mask, c) if axis == "row" else (r, c ^ mask)
                result.append((r * self.cols + c, r2 * self.cols + c2))
        return result

    def bit(self, step):
        values = [((self.row_at if axis == "row" else self.col_at) & mask) != 0 for axis, mask in step]
        return jnp.where(self.core == 0, values[0], values[1]).astype(jnp.int32)

    def swap(self, block, step):
        return lax.ppermute(block, AXES, self.pairs(step))

    def open(self, sent, kept):
        return Sum(self, sent, kept)


class Sum:
    def __init__(self, reducer, sent, kept):
        self.reducer = reducer
        self.sent, self.kept, self.got = sent, kept, None
        count = len(reducer.steps)
        self.plan = [reducer.core_step] + reducer.steps + reducer.steps[-2::-1] + [reducer.core_step]
        self.halvings = count
        self.stage = 0

    @property
    def done(self):
        return self.stage == len(self.plan)

    def swap(self):
        self.got = self.reducer.swap(self.sent, self.plan[self.stage])

    def combine(self):
        sent, kept, got, stage = self.sent, self.kept, self.got, self.stage
        self.stage += 1
        self.got = None
        steps = self.reducer.steps
        if stage < self.halvings - 1:
            bit = self.reducer.bit(steps[stage])
            half = kept.shape[0] // 2

            def summed(at):
                pieces = [lax.dynamic_slice_in_dim(a, at * half, half, 0).astype(F32) for a in (kept, got)]
                return (pieces[0] + pieces[1]).astype(BF16)

            self.sent, self.kept = summed(1 - bit), summed(bit)
        elif stage <= self.halvings:
            self.sent = self.kept = (kept.astype(F32) + got.astype(F32)).astype(BF16)
        elif not self.done:
            bit = self.reducer.bit(self.plan[stage]) == 1
            self.sent = self.kept = jnp.concatenate([jnp.where(bit, got, kept), jnp.where(bit, kept, got)], axis=0)
        else:
            self.got = got

    def advance(self):
        self.swap()
        self.combine()


def shift_pairs(count):
    forward = [(i, i + 1) for i in range(count - 1)]
    return forward, [(b, a) for a, b in forward]


def on_device(
    activations, gain_first, shift_first, in_weight, conv_kernel, mix_first, mix_second, mix_third,
    mix_fourth, out_weight, scale_mixer, gain_second, shift_second, up_weight, up_bias, down_weight,
    scale_mlp, valid_pixels, tile_images, cotangent,
):
    tile_rows, tile_cols, width = activations.shape
    pixels = tile_rows * tile_cols
    hidden = up_weight.shape[1]
    gate_count = conv_kernel.shape[-1]
    joined_count = in_weight.shape[1]
    lead_count = joined_count - gate_count
    span = tile_cols + 8
    ext_rows = tile_rows + 2 * HALO
    ext_pixels = ext_rows * span
    tab = tables()
    down_pairs, up_pairs = shift_pairs(lax.axis_size("row"))
    right_pairs, left_pairs = shift_pairs(lax.axis_size("col"))

    row_at, col_at = lax.axis_index("row"), lax.axis_index("col")
    row_last, col_last = lax.axis_size("row") - 1, lax.axis_size("col") - 1
    own_image = tile_images[row_at, col_at]

    def same(row, col, inside):
        return jnp.logical_and(inside, tile_images[row, col] == own_image)

    same_up = same(jnp.maximum(row_at - 1, 0), col_at, row_at > 0)
    same_down = same(jnp.minimum(row_at + 1, row_last), col_at, row_at < row_last)
    same_left = same(row_at, jnp.maximum(col_at - 1, 0), col_at > 0)
    same_right = same(row_at, jnp.minimum(col_at + 1, col_last), col_at < col_last)

    def rows_around(block):
        return lax.ppermute(block[-HALO:], "row", down_pairs), lax.ppermute(block[:HALO], "row", up_pairs)

    def cols_around(above, below, block):
        def side(cols):
            return jnp.concatenate([above[:, cols], block[:, cols], below[:, cols]], axis=0)

        last, first = slice(tile_cols - HALO, tile_cols), slice(0, HALO)
        return lax.ppermute(side(last), "col", right_pairs), lax.ppermute(side(first), "col", left_pairs)

    near = jnp.stack([same_up, same_down, same_left, same_right]).astype(jnp.int32)

    def masked(pair, marks, outside):
        return tuple(jnp.where(mark, block, jnp.asarray(outside, BF16)) for block, mark in zip(pair, marks))

    def flat(block):
        return block.reshape(block.shape[0] * block.shape[1], block.shape[2])

    marked = jnp.where(valid_pixels[..., None] != 0, activations, jnp.asarray(OUTSIDE, BF16))
    taps = jnp.pad(conv_kernel.astype(F32).reshape(TAPS * TAPS, gate_count), ((0, 0), (lead_count, 0)))
    spec = jnp.dot(tab["spectrum"], taps, precision=lax.Precision.HIGHEST, preferred_element_type=F32)
    w1 = jnp.zeros((128, 128), BF16).at[32:64, 64:128].set(mix_first)
    w2 = jnp.zeros((128, 128), BF16).at[64:128, :].set(mix_second)
    above, below = rows_around(marked)
    (above, below, spec, w1, w2, valid_pixels) = lax.optimization_barrier(
        (above, below, spec, w1, w2, valid_pixels)
    )
    left, right = cols_around(*masked((above, below), (same_up, same_down), OUTSIDE), marked)

    x_own = activations.reshape(pixels, width)
    cot = cotangent.reshape(pixels, width)
    valid = valid_pixels.astype(F32).reshape(pixels, 1)
    vecs = jnp.stack(
        [gain_first, shift_first, scale_mixer, gain_second, shift_second, scale_mlp, scale_mlp, scale_mlp]
    ).astype(F32)
    bias = up_bias.astype(F32).reshape(1, hidden)
    w3, w4 = mix_third, mix_fourth
    (left, right, valid, vecs, bias) = lax.optimization_barrier((left, right, valid, vecs, bias))
    x_source = flat(above), flat(marked), flat(below), left, right

    chunk = OUT * tile_cols
    steps = tile_rows // OUT
    anywhere = pl.BlockSpec(memory_space=pl.ANY)
    in_smem = pl.BlockSpec(memory_space=pltpu.SMEM)
    (
        xwaves, spread, prods, lead, middle, active, slope, grad_down,
    ) = pl.pallas_call(
        forward_kernel,
        grid=(steps,),
        in_specs=[
            in_smem,
            chunked((chunk, width)), chunked((chunk, 1)), chunked((chunk, width)), whole((8, width)),
            whole((1, hidden)), whole((128, 128)), whole((128, 128)), whole(w3.shape), whole(tab["window"].shape),
            whole(tab["tile_back"].shape),
            whole((HALO * tile_cols, width)), whole((pixels, width)), whole((HALO * tile_cols, width)),
            whole((ext_rows, HALO, width)), whole((ext_rows, HALO, width)),
        ] + [anywhere] * 5,
        out_specs=[
            anywhere, anywhere, anywhere, chunked((chunk, 128)), chunked((chunk, width)), anywhere, anywhere, anywhere,
        ],
        out_shape=[
            shaped((steps * 2 * SLOTS * TILES, joined_count), BF16), shaped((pixels, joined_count), F32),
            shaped((pixels, joined_count), F32), shaped((pixels, 128), F32),
            shaped((pixels, width), F32), shaped((pixels, hidden), BF16), shaped((pixels, hidden), BF16),
            shaped((hidden, width), BF16),
        ],
        scratch_shapes=[
            pltpu.VMEM((ext_pixels, joined_count + 128), F32),
            pltpu.VMEM((2 * SLOTS, LANES * TILES), F32), pltpu.VMEM((2 * SLOTS, LANES * TILES), BF16),
            pltpu.VMEM((pixels, hidden), BF16), pltpu.VMEM((pixels, width), BF16),
            pltpu.VMEM((ext_rows * tile_cols, width), F32), pltpu.VMEM((ext_pixels, width), F32),
            pltpu.VMEM((width, joined_count), BF16),
            pltpu.VMEM((3 * SLOTS, joined_count), F32), pltpu.VMEM(w4.shape, BF16), pltpu.VMEM((width, width), BF16),
            pltpu.VMEM((width, hidden), BF16), pltpu.VMEM((2, 2 * SLOTS * TILES, joined_count), BF16),
            pltpu.VMEM((2, chunk, joined_count), F32), pltpu.VMEM((2, chunk, joined_count), F32),
            pltpu.VMEM((2, chunk, hidden), BF16), pltpu.VMEM((hidden, width), BF16),
            pltpu.SemaphoreType.DMA((5,)), pltpu.SemaphoreType.DMA((2,)), pltpu.SemaphoreType.DMA((2,)),
            pltpu.SemaphoreType.DMA((2,)), pltpu.SemaphoreType.DMA((2,)), pltpu.SemaphoreType.DMA((steps,)),
            pltpu.SemaphoreType.DMA((4,)),
        ],
        compiler_params=params(58),
        cost_estimate=cost(30),
        name="forward",
    )(
        near, x_own, valid, cot, vecs, bias, w1, w2, w3, tab["window"], tab["tile_back"],
        *x_source, in_weight, spec, w4, out_weight, up_weight,
    )

    rows = 256
    count = pixels // rows
    wide = 640
    few = pixels // wide
    early = hidden + width
    late = 576
    gmiddle, ffn_sent, ffn_kept, ffn_sums, bias_sum = pl.pallas_call(
        ffn_back_kernel,
        grid=(few,),
        in_specs=[
            chunked((wide, width)), chunked((wide, hidden)), chunked((wide, width)), chunked((wide, 1)),
            whole((8, width)), whole((hidden, width)), whole((width, hidden)), whole((hidden, width)),
        ],
        out_specs=[
            chunked((wide, width)), held((early, width)), held((early, width)), held((8, width)),
            held((8, hidden)),
        ],
        out_shape=[
            shaped((pixels, width), F32), shaped((early, width), BF16), shaped((early, width), BF16),
            shaped((8, width), F32),
            shaped((8, hidden), F32),
        ],
        scratch_shapes=[pltpu.VMEM((pixels, width), BF16), pltpu.VMEM((pixels, hidden), BF16)],
        compiler_params=params(48),
        cost_estimate=cost(16),
        name="ffn_back",
    )(cot, slope, middle, valid, vecs, down_weight, up_weight, grad_down)

    gspread, glead, ffn_sent, ffn_kept = pl.pallas_call(
        mixer_back_kernel,
        grid=(few,),
        in_specs=[
            chunked((wide, width)), chunked((wide, joined_count)), chunked((wide, joined_count)),
            chunked((wide, 128)), whole((8, width)), whole((128, 128)), whole((128, 128)), whole(w3.shape),
            whole(w4.shape), whole((width, width)), anywhere, anywhere,
        ],
        out_specs=[chunked((wide, joined_count)), chunked((wide, 128)), anywhere, anywhere],
        out_shape=[
            shaped((pixels, joined_count), BF16), shaped((pixels, 128), F32), shaped((early, width), BF16),
            shaped((early, width), BF16),
        ],
        input_output_aliases={10: 2, 11: 3},
        scratch_shapes=[
            pltpu.VMEM((width, width), F32), pltpu.VMEM(w4.shape, F32), pltpu.VMEM(w3.shape, F32),
            pltpu.VMEM((128, 128), F32), pltpu.VMEM((128, 128), F32), pltpu.VMEM((2 * width, width), BF16),
            pltpu.SemaphoreType.DMA((2,)),
        ],
        compiler_params=params(48),
        cost_estimate=cost(9),
        name="mixer_back",
    )(gmiddle, spread, prods, lead, vecs, w1, w2, w3, w4, out_weight, ffn_sent, ffn_kept)

    reducer = Reducer()
    ffn = reducer.open(ffn_sent, ffn_kept)
    ffn.swap()
    tie = lax.optimization_barrier
    block = gspread.reshape(tile_rows, tile_cols, joined_count)
    above, below = rows_around(block)
    grad_kernel = pl.pallas_call(
        kernel_back_kernel,
        grid=(steps,),
        in_specs=[
            chunked((2 * SLOTS * TILES, joined_count)), chunked((chunk, joined_count)),
            whole(tab["tile"].shape), whole(tab["kernel_back"].shape),
        ],
        out_specs=held((112, width)),
        out_shape=shaped((112, width), BF16),
        scratch_shapes=[
            pltpu.VMEM((chunk, joined_count), F32), pltpu.VMEM((2 * SLOTS, LANES * TILES), F32),
            pltpu.VMEM((4 * SLOTS, joined_count), F32),
        ],
        compiler_params=params(48),
        cost_estimate=cost(9),
        name="kernel_back",
    )(xwaves, gspread, tab["tile"], tab["kernel_back"])
    (above, below, grad_kernel, ffn.kept, ffn.got) = tie((above, below, grad_kernel, ffn.kept, ffn.got))
    left, right = cols_around(*masked((above, below), (same_up, same_down), 0.0), block)
    ffn.combine()
    (left, right, ffn.sent, ffn.kept) = tie((left, right, ffn.sent, ffn.kept))
    ffn.swap()
    above, below = flat(above), flat(below)

    gjoined = pl.pallas_call(
        gates_back_kernel,
        grid=(steps,),
        in_specs=[
            in_smem,
            whole((HALO * tile_cols, joined_count)), whole((pixels, joined_count)),
            whole((HALO * tile_cols, joined_count)), whole((ext_rows, HALO, joined_count)),
            whole((ext_rows, HALO, joined_count)), chunked((chunk, 128)),
            pl.BlockSpec((3 * SLOTS, joined_count), lambda i: (1, 0), pipeline_mode=pl.Buffered(1)),
            whole(tab["window"].shape), whole(tab["tile_back"].shape),
        ],
        out_specs=chunked((chunk, joined_count)),
        out_shape=shaped((pixels, joined_count), BF16),
        scratch_shapes=[
            pltpu.VMEM((ext_rows * tile_cols, joined_count), F32), pltpu.VMEM((ext_pixels, joined_count), F32), pltpu.VMEM((2 * SLOTS, LANES * TILES), F32),
            pltpu.VMEM((2 * SLOTS, LANES * TILES), BF16), pltpu.VMEM((chunk, joined_count), F32),
        ],
        compiler_params=params(48),
        cost_estimate=cost(11),
        name="gates_back",
    )(near, above, gspread, below, left, right, glead, spec, tab["window"], tab["tile_back"])
    (gjoined, ffn.got) = tie((gjoined, ffn.got))
    ffn.combine()
    (gjoined, ffn.sent, ffn.kept) = tie((gjoined, ffn.sent, ffn.kept))
    ffn.swap()

    ginput, rest_sent, rest_kept = pl.pallas_call(
        in_back_kernel,
        grid=(few,),
        in_specs=[
            chunked((wide, joined_count)), chunked((wide, width)), chunked((wide, width)), chunked((wide, 1)),
            whole((8, width)), whole((width, joined_count)), whole((112, width)),
            whole((8, width)), whole((8, hidden)),
        ],
        out_specs=[chunked((wide, width)), held((late, width)), held((late, width))],
        out_shape=[
            shaped((pixels, width), BF16), shaped((late, width), BF16), shaped((late, width), BF16),
        ],
        scratch_shapes=[
            pltpu.VMEM((pixels, width), BF16), pltpu.VMEM((pixels, joined_count), BF16), pltpu.VMEM((8, width), F32),
        ],
        compiler_params=params(48),
        cost_estimate=cost(8),
        name="in_back",
    )(
        gjoined, x_own, gmiddle, valid, vecs, in_weight, grad_kernel, ffn_sums, bias_sum,
    )
    rest = reducer.open(rest_sent, rest_kept)
    rest.swap()
    (rest.kept, ffn.got) = tie((rest.kept, ffn.got))
    ffn.combine()
    ffn.swap()

    def down(active, before, first, blocks):
        return pl.pallas_call(
            down_kernel,
            grid=(blocks,),
            in_specs=[
                pl.BlockSpec((rows, hidden), lambda i: (i + first, 0)),
                pl.BlockSpec((rows, width), lambda i: (i + first, 0)), whole((8, width)), whole((hidden, width)),
                pl.BlockSpec(memory_space=pl.ANY),
            ],
            out_specs=pl.BlockSpec((rows, width), lambda i: (i + first, 0)),
            out_shape=shaped((pixels, width), BF16),
            input_output_aliases={4: 0} if first else {},
            compiler_params=params(48),
            cost_estimate=cost(4),
            name="down",
        )(active, middle, vecs, down_weight, before)

    (active, rest.sent, ffn.sent) = tie((active, rest.sent, ffn.sent))
    outputs = down(active, jnp.zeros((8, 128), BF16), 0, count // 2)

    def onward(way, *others):
        values = tie((way.kept, way.got) + others)
        way.kept, way.got = values[:2]
        way.combine()
        if not way.done:
            way.swap()
        return values[2:]

    (outputs,) = onward(rest, outputs)
    (rest.kept,) = onward(ffn, rest.kept)
    (outputs, rest.sent, ffn.sent) = tie((outputs, rest.sent, ffn.sent))
    outputs = down(active, outputs, count // 2, count - count // 2)
    (outputs,) = onward(rest, outputs)
    vector = shaped((1, width), F32)
    block_at = lambda i: (jnp.minimum(i, 3), 0)
    expand_early = pl.pallas_call(
        expand_early_kernel,
        grid=(5,),
        in_specs=[
            chunked((width, width)), chunked((width, width)), pl.BlockSpec((width, width), block_at),
            whole((width, width)), whole((8, width)),
        ],
        out_specs=[
            pl.BlockSpec((width, width), block_at), pl.BlockSpec((width, width), lambda i: (0, jnp.minimum(i, 3))),
            held((1, width)), held((width, width)), held(w4.shape), held(w3.shape), held(mix_second.shape),
            held(mix_first.shape), held((1, width)),
        ],
        out_shape=[
            shaped((hidden, width), F32), shaped((width, hidden), F32), vector, shaped((width, width), F32),
            shaped(w4.shape, F32), shaped(w3.shape, F32), shaped(mix_second.shape, F32),
            shaped(mix_first.shape, F32), vector,
        ],
        compiler_params=params(32),
        cost_estimate=cost(5),
        name="expand_early",
    )
    expanded = None
    for who in "frfrrfrrfrfr":
        way, other = (ffn, rest) if who == "f" else (rest, ffn)
        if not way.done:
            (other.kept,) = onward(way, other.kept)
        if ffn.done and expanded is None:
            expanded = expand_early(ffn.kept, ffn.got, down_weight, out_weight, vecs)
            (rest.kept, expanded) = tie((rest.kept, expanded))
    while not (ffn.done and rest.done):
        for way in (ffn, rest):
            if not way.done:
                onward(way)
    if expanded is None:
        expanded = expand_early(ffn.kept, ffn.got, down_weight, out_weight, vecs)
    (grad_down_weight, grad_up_weight, scale_2, grad_out, grad_4, grad_3, grad_2, grad_1, scale_1) = expanded
    grad_in_weight, grad_conv, gain_1, shift_1, gain_2, shift_2, grad_bias = pl.pallas_call(
        expand_late_kernel,
        in_specs=[pl.BlockSpec(memory_space=pltpu.VMEM)] * 2,
        out_specs=[pl.BlockSpec(memory_space=pltpu.VMEM)] * 7,
        out_shape=[
            shaped(in_weight.shape, F32), shaped(conv_kernel.shape, F32), vector, vector, vector, vector,
            shaped((1, hidden), F32),
        ],
        compiler_params=pltpu.CompilerParams(vmem_limit_bytes=32 * 1024 * 1024),
        cost_estimate=cost(3),
        name="expand_late",
    )(rest.kept, rest.got)
    return (
        outputs.reshape(activations.shape),
        ginput.reshape(activations.shape),
        gain_1.reshape(width),
        shift_1.reshape(width),
        grad_in_weight,
        grad_conv,
        grad_1,
        grad_2,
        grad_3,
        grad_4,
        grad_out,
        scale_1.reshape(width),
        gain_2.reshape(width),
        shift_2.reshape(width),
        grad_up_weight,
        grad_bias.reshape(hidden),
        grad_down_weight,
        scale_2.reshape(width),
    )


def solution(mesh):
    tiles = P("row", "col", None)
    in_specs = (tiles,) + (P(),) * 16 + (P("row", "col"), P(), tiles)
    out_specs = (tiles, tiles) + (P(),) * 16
    return jax.shard_map(on_device, mesh=mesh, in_specs=in_specs, out_specs=out_specs, check_vma=False)
```

```python
import math
from functools import partial

import jax
import jax.numpy as jnp
import ml_dtypes
import numpy as np
from jax import lax
from jax.experimental import pallas as pl
from jax.experimental.pallas import tpu as pltpu
from jax.sharding import PartitionSpec as P

EPS = 1e-06
TAPS = 7
HALO = 3
OUT = 8
WIN = OUT + TAPS - 1
PITCH = 16
SLOTS = 112
OUTSIDE = 64.0
COS_SCALE = 1.422015
SIN_SCALE = 1.818765
TILES = 5
LANES = 512
BF16 = jnp.bfloat16
F32 = jnp.float32


def frequencies():
    pairs, own, seen = [], [], set()
    for u in range(WIN):
        for v in range(WIN):
            if (u, v) in seen:
                continue
            twin = ((-u) % WIN, (-v) % WIN)
            seen.update([(u, v), twin])
            (own if twin == (u, v) else pairs).append((u, v))
    return np.array(pairs + own), np.array([2.0] * len(pairs) + [1.0] * len(own))


def angles(rows, cols, pitch):
    freq, _ = frequencies()
    a = np.arange(rows)[:, None]
    b = np.arange(pitch)[None, :]
    theta = 2 * np.pi * (freq[:, 0, None, None] * a + freq[:, 1, None, None] * b) / WIN
    live = np.broadcast_to(b < cols, (rows, pitch))
    cos = np.zeros((SLOTS, rows * pitch))
    sin = np.zeros((SLOTS, rows * pitch))
    cos[: len(freq)] = (np.cos(theta) * live).reshape(len(freq), -1)
    sin[: len(freq)] = (np.sin(theta) * live).reshape(len(freq), -1)
    return cos, sin


def tables():
    _, weight = frequencies()
    weight = np.concatenate([weight, np.zeros(SLOTS - len(weight))])[:, None]
    area = WIN * WIN

    def ahead(cos, sin):
        return np.concatenate([COS_SCALE * cos, -SIN_SCALE * sin])

    def back(cos, sin):
        return np.concatenate([weight * COS_SCALE * cos, -weight * SIN_SCALE * sin]).T

    window = angles(WIN, WIN, PITCH)
    tile = angles(OUT, OUT, OUT)
    cos, sin = angles(TAPS, TAPS, TAPS)
    third = 1.0 / 3.0
    spectrum = np.concatenate(
        [
            cos * (third / (area * COS_SCALE**2)),
            -sin * (third / (area * COS_SCALE * SIN_SCALE)),
            cos * (third / (area * SIN_SCALE**2)),
        ]
    )
    wide = weight * third / area
    kernel_back = np.concatenate(
        [
            wide * cos / COS_SCALE**2,
            wide * cos / SIN_SCALE**2,
            -wide * sin / (COS_SCALE * SIN_SCALE),
            wide * sin / (COS_SCALE * SIN_SCALE),
        ]
    ).T
    kernel_back = np.concatenate([kernel_back, np.zeros((7, 4 * SLOTS))])
    half = ml_dtypes.bfloat16
    return dict(
        window=ahead(*window).astype(half),
        tile=ahead(*tile).astype(half),
        window_back=back(*window).astype(half),
        tile_back=back(*tile).astype(half),
        spectrum=np.concatenate([spectrum, spectrum[:, ::-1]]).astype(np.float32),
        kernel_back=kernel_back.astype(np.float32),
    )


def dot(left, right):
    return jnp.dot(left, right, preferred_element_type=F32)


def dot_right(left, right):
    return lax.dot_general(left, right, (((1,), (1,)), ((), ())), preferred_element_type=F32)


def dot_left(left, right):
    return lax.dot_general(left, right, (((0,), (0,)), ((), ())), preferred_element_type=F32)


def normalize(values):
    center = values - jnp.mean(values, axis=-1, keepdims=True)
    inverse = lax.rsqrt(jnp.mean(center * center, axis=-1, keepdims=True) + EPS)
    return center * inverse, inverse


def norm_back(masked, normal, inverse, gain):
    scaled = masked * gain
    centered = scaled - jnp.mean(scaled, axis=-1, keepdims=True)
    return inverse * (centered - normal * jnp.mean(scaled * normal, axis=-1, keepdims=True))


def gelu_pair(x):
    cumulative = 0.5 + 0.5 * lax.erf(x * math.sqrt(0.5))
    density = jnp.exp(-0.5 * x * x) * (1.0 / math.sqrt(2.0 * math.pi))
    return x * cumulative, cumulative + x * density


UP, DOWN, LEFT, RIGHT = range(4)


def fill(source, near, outside, above, own, below):
    edge, body = above.shape[0], own.shape[0]
    source[0:edge, :] = jnp.where(near[UP] != 0, above[...].astype(F32), outside)
    source[edge : edge + body, :] = own[...].astype(F32)
    source[edge + body : 2 * edge + body, :] = jnp.where(near[DOWN] != 0, below[...].astype(F32), outside)


def widen(ext, lanes, near, outside, source, left, right, first_row, rows):
    for r in range(rows):
        row = first_row + r
        line = source[pl.ds(pl.multiple_of(row * 40, 8), 40), :]
        depth = line.shape[1]
        before = jnp.where(near[LEFT] != 0, left[row].astype(F32), outside)
        after = jnp.where(near[RIGHT] != 0, right[row].astype(F32), outside)
        pieces = [before, line, after, jnp.full((2, depth), outside, F32)]
        ext[pl.ds(pl.multiple_of(row * 48, 8), 48), lanes] = jnp.concatenate(pieces, axis=0)


def depthwise(ext, first_row, spec, tx, ty, waves, mixed_waves, result_ref, kept=None):
    span = 48

    def block_of_lanes(block, carry):
        lanes = pl.ds(pl.multiple_of(LANES * block, LANES), LANES)
        window = jnp.concatenate(
            [
                jnp.concatenate(
                    [
                        ext[pl.ds(pl.multiple_of((first_row + r) * span + OUT * col, 8), PITCH), lanes]
                        for r in range(WIN)
                    ],
                    axis=0,
                ).astype(BF16)
                for col in range(TILES)
            ],
            axis=1,
        )
        waves[...] = dot(tx[...], window)
        for row in range(0, SLOTS, 16):
            here, there = slice(row, row + 16), slice(SLOTS + row, SLOTS + row + 16)
            low, cross, high = (spec[pl.ds(SLOTS * k + row, 16), lanes] for k in range(3))
            for col in range(TILES):
                at = slice(LANES * col, LANES * col + LANES)
                real, imag = waves[here, at], waves[there, at]
                mixed_waves[here, at] = (low * real + cross * imag).astype(BF16)
                mixed_waves[there, at] = (high * imag - cross * real).astype(BF16)
                if kept is not None:
                    base = 2 * SLOTS * col + row
                    kept[base : base + 16, lanes] = real.astype(BF16)
                    kept[base + SLOTS : base + SLOTS + 16, lanes] = imag.astype(BF16)
        result = dot(ty[...], mixed_waves[...])
        for col in range(TILES):
            for r in range(OUT):
                result_ref[r * 40 + OUT * col : r * 40 + OUT * col + OUT, lanes] = result[
                    OUT * r : OUT * r + OUT, LANES * col : LANES * col + LANES
                ]
        return carry

    lax.fori_loop(0, 1024 // LANES, block_of_lanes, 0)


GAIN_1, SHIFT_1, SCALE_1, GAIN_2, SHIFT_2, SCALE_2 = range(6)


def copies(pairs, sems):
    return [pltpu.make_async_copy(src, dst, sems.at[k]) for k, (src, dst) in enumerate(pairs)]


class Sender:
    def __init__(self, hbm, held, sems, step, rows):
        self.hbm, self.held, self.sems, self.step, self.rows = hbm, held, sems, step, rows
        self.own = held.shape[0] > rows
        self.ref = held.at[self.at(step), :] if self.own else held

    def at(self, step):
        return pl.ds(pl.multiple_of(step * self.rows, 16), self.rows)

    def copy(self, step):
        source = self.held.at[self.at(step), :] if self.own else self.held
        return pltpu.make_async_copy(source, self.hbm.at[self.at(step), :], self.sems.at[step])

    def free(self):
        if not self.own:
            pl.when(self.step > 0)(lambda: self.copy(self.step - 1).wait())

    def start(self):
        self.copy(self.step).start()

    def finish(self):
        if self.own:
            for step in range(self.sems.shape[0]):
                self.copy(step).wait()
        else:
            self.copy(self.step).wait()


def forward_kernel(
    near, x_own, valid, cot, vecs, up_bias, w1, w2, w3, tx, ty,
    x_above, x_marked, x_below, x_left, x_right, in_hbm, spec_hbm, w4_hbm, out_hbm, up_hbm, down_hbm,
    waves_hbm, spread_hbm, prods_hbm, lead_out, middle_hbm, active_hbm, gmiddle_hbm, sent, kept, vec_sums, bias_sum,
    ext, waves, mixed_waves, active_all, gdown_all, normed_all, slope_all, middle_all,
    x_source, x_ext, in_w, spec, w4, out_w, up_w, down_w, waves_held, spread_held, prods_held, grad_down, grad_up,
    in_sems, waves_sems, spread_sems, prods_sems, middle_sems, active_sems, gmiddle_sems, down_sems, up_sems,
):
    step = pl.program_id(0)
    last = pl.num_programs(0) - 1
    span = 48
    chunk = lead_out.shape[0]
    gain = vecs[GAIN_1 : GAIN_1 + 1, :]
    shift = vecs[SHIFT_1 : SHIFT_1 + 1, :]
    loads = copies(
        [(in_hbm, in_w), (spec_hbm.at[: 3 * SLOTS, :], spec), (w4_hbm, w4), (out_hbm, out_w), (up_hbm, up_w), (down_hbm, down_w)],
        in_sems,
    )

    def begin():
        for load in loads:
            load.start()

    pl.when(step == 0)(begin)

    def arrived(*which):
        def wait():
            for k in which:
                loads[k].wait()

        pl.when(step == 0)(wait)

    waves_to = Sender(waves_hbm, waves_held, waves_sems, step, waves_held.shape[0])
    spread_to = Sender(spread_hbm, spread_held, spread_sems, step, chunk)
    prods_to = Sender(prods_hbm, prods_held, prods_sems, step, chunk)
    middle_to = Sender(middle_hbm, middle_all, middle_sems, step, chunk)
    active_to = Sender(active_hbm, active_all, active_sems, step, chunk)
    spread, prods = spread_held, prods_held
    rows = pl.ds(pl.multiple_of(step * chunk, 16), chunk)

    def project(start, rows):
        at = pl.ds(start, rows)
        values = x_ext[at, :]
        normal, _ = normalize(values)
        normed = jnp.where(values[:, :1] < 0.5 * OUTSIDE, normal * gain + shift, 0.0).astype(BF16)
        for block in range(2):
            lanes = slice(512 * block, 512 * block + 512)
            joined = dot(normed, in_w[:, lanes])
            if block == 0:
                ext[at, 1024:1152] = joined[:, :128]
            low = joined.astype(BF16)
            ext[at, lanes] = low.astype(F32)

    arrived(0)

    @pl.when(step == 0)
    def _():
        fill(x_source, near, OUTSIDE, x_above, x_marked, x_below)
        widen(x_ext, slice(0, 512), near, OUTSIDE, x_source, x_left, x_right, 0, 6)
        project(0, 6 * span)

    widen(x_ext, slice(0, 512), near, OUTSIDE, x_source, x_left, x_right, OUT * step + 6, OUT)

    project(pl.multiple_of((OUT * step + 6) * span, 16), OUT * span)

    arrived(1)
    waves_to.free()
    spread_to.free()
    depthwise(ext, OUT * step, spec, tx, ty, waves, mixed_waves, spread, waves_held)
    waves_to.start()
    spread_to.start()

    lead = jnp.concatenate(
        [
            ext[pl.ds(pl.multiple_of((OUT * step + HALO + r) * span, 8), span), 1024:1152][HALO : HALO + 40]
            for r in range(OUT)
        ],
        axis=0,
    )
    lead = pltpu.roll(lead, 32, 1)
    lead_out[...] = lead
    mixed = lead * spread[:, :128]
    arrived(2, 3)
    prods_to.free()
    for weight, lo, hi in ((w1, 0, 128), (w2, 128, 256), (w3, 256, 512), (w4, 512, 1024)):
        produced = dot(mixed.astype(BF16), weight[...])
        prods[:, lo:hi] = produced
        mixed = produced * spread[:, lo:hi]
    prods_to.start()
    branch = dot(mixed.astype(BF16), out_w[...])
    middle = x_own[...].astype(F32) + vecs[SCALE_1 : SCALE_1 + 1, :] * branch
    middle_all[rows, :] = middle
    middle_to.start()
    normal, _ = normalize(middle)
    gain_2 = vecs[GAIN_2 : GAIN_2 + 1, :]
    normed = ((normal * gain_2 + vecs[SHIFT_2 : SHIFT_2 + 1, :]) * valid[rows, :]).astype(BF16)
    normed_all[rows, :] = normed
    arrived(4, 5)
    for block in range(4):
        lanes = slice(512 * block, 512 * block + 512)
        pre = dot(normed, up_w[:, lanes]) + up_bias[:, lanes]
        active, slope = gelu_pair(pre)
        active_all[rows, lanes] = active.astype(BF16)
        slope_all[rows, lanes] = slope.astype(BF16)
    active_to.start()
    gdown_all[rows, :] = (cot[rows, :].astype(F32) * vecs[SCALE_2 : SCALE_2 + 1, :]).astype(BF16)

    @pl.when(step == last)
    def _():
        even = lax.axis_index("col") % 2 == 0

        def part(source, to, block, sems):
            lanes = slice(512 * block, 512 * block + 512)
            return pltpu.make_async_copy(source.at[lanes, :], to.at[lanes, :], sems.at[block])

        def both(act):
            pl.when(even)(lambda: act(sent, kept))
            pl.when(jnp.logical_not(even))(lambda: act(kept, sent))

        for block in range(4):
            lanes = slice(512 * block, 512 * block + 512)
            grad_down[lanes, :] = dot_left(gdown_all[...], active_all[:, lanes]).astype(BF16)

        def send_down(for_up, for_down):
            for block in range(4):
                part(grad_down, for_down, block, down_sems).start()

        both(send_down)

        gmiddle = x_source
        vec_sums[...] = jnp.zeros_like(vec_sums)
        bias_sum[...] = jnp.zeros_like(bias_sum)
        pixels = gdown_all.shape[0]
        half = pixels // 2
        for k in range(2):
            here = slice(half * k, half * k + half)
            gnormed = jnp.zeros((half, 512), F32)
            for block in range(4):
                lanes = slice(512 * block, 512 * block + 512)
                gactive = dot_right(gdown_all[here, :], down_w[lanes, :])
                gpre = (gactive * slope_all[here, lanes].astype(F32)).astype(BF16)
                slope_all[here, lanes] = gpre
                bias_sum[0:1, lanes] += jnp.sum(gpre.astype(F32), axis=0, keepdims=True)
                gnormed = gnormed + dot_right(gpre, up_w[:, lanes])
            normal, inverse = normalize(middle_all[here, :])
            masked = gnormed * valid[here, :]
            vec_sums[0:1, :] += jnp.sum(masked * normal, axis=0, keepdims=True)
            vec_sums[1:2, :] += jnp.sum(masked, axis=0, keepdims=True)
            gmiddle[here, :] = cot[here, :].astype(F32) + norm_back(masked, normal, inverse, gain_2)
            pltpu.make_async_copy(gmiddle.at[here, :], gmiddle_hbm.at[here, :], gmiddle_sems.at[k]).start()
        for block in range(4):
            lanes = slice(512 * block, 512 * block + 512)
            grad_up[lanes, :] = dot_left(normed_all[...], slope_all[:, lanes]).astype(BF16)
            both(lambda for_up, for_down, block=block: part(grad_up, for_up, block, up_sems).start())
        for sender in (waves_to, spread_to, prods_to, middle_to, active_to):
            sender.finish()
        for k in range(2):
            here = slice(half * k, half * k + half)
            pltpu.make_async_copy(gmiddle.at[here, :], gmiddle_hbm.at[here, :], gmiddle_sems.at[k]).wait()

        def finish(for_up, for_down):
            for block in range(4):
                part(grad_down, for_down, block, down_sems).wait()
                part(grad_up, for_up, block, up_sems).wait()

        both(finish)


def mixer_back_kernel(
    gmiddle, spread, prods, lead, vecs, w1, w2, w3, w4, out_w, sent_before, kept_before,
    gspread, glead, sent, kept,
    d_out, d_4, d_3, d_2, d_1, grads, sems,
):
    step = pl.program_id(0)

    @pl.when(step == 0)
    def _():
        for total in (d_out, d_4, d_3, d_2, d_1):
            total[...] = jnp.zeros_like(total)

    grad = gmiddle[...]
    glow = (grad * vecs[SCALE_1 : SCALE_1 + 1, :]).astype(BF16)
    part, prod = spread[:, 512:1024], prods[:, 512:1024]
    d_out[...] += dot_left((prod * part).astype(BF16), glow)
    gmixed = dot_right(glow, out_w[...])
    for weight, total, lo, hi, below in (
        (w4, d_4, 512, 1024, 256), (w3, d_3, 256, 512, 128), (w2, d_2, 128, 256, 0)
    ):
        gspread[:, lo:hi] = (gmixed * prods[:, lo:hi]).astype(BF16)
        gprod = (gmixed * spread[:, lo:hi]).astype(BF16)
        mixed = (prods[:, below:lo] * spread[:, below:lo]).astype(BF16)
        total[...] += dot_left(mixed, gprod)
        gmixed = dot_right(gprod, weight[...])
    part, prod, head = spread[:, :128], prods[:, :128], lead[...]
    gprod = (gmixed * part).astype(BF16)
    d_1[...] += dot_left((head * part).astype(BF16), gprod)
    gfirst = dot_right(gprod, w1[...])
    gspread[:, :128] = (gmixed * prod + gfirst * head).astype(BF16)
    glead[...] = pltpu.roll(gfirst * part, 96, 1)

    @pl.when(step == pl.num_programs(0) - 1)
    def _():
        grads[0:448, :] = d_out[0:448, :].astype(BF16)
        grads[448:512, :] = jnp.zeros((64, 512), BF16)
        grads[512:576, :] = d_out[448:512, :].astype(BF16)
        grads[576:832, :] = d_4[...].astype(BF16)
        grads[832:960, 0:256] = d_3[...].astype(BF16)
        grads[832:960, 256:384] = d_2[...].astype(BF16)
        grads[832:960, 384:512] = d_1[...].astype(BF16)
        grads[960:1024, :] = jnp.zeros((64, 512), BF16)
        start = sent.shape[0] - 512

        def finish(first, second):
            parts = copies(
                [
                    (grads.at[0:512, :], first.at[start : start + 512, :]),
                    (grads.at[512:1024, :], second.at[start : start + 512, :]),
                ],
                sems,
            )
            for part in parts:
                part.start()
            for part in parts:
                part.wait()

        even = lax.axis_index("col") % 2 == 0
        pl.when(even)(lambda: finish(kept, sent))
        pl.when(jnp.logical_not(even))(lambda: finish(sent, kept))


def down_kernel(active, middle, vecs, down_w, before, outputs):
    down = dot(active[...], down_w[...])
    outputs[...] = (middle[...] + vecs[SCALE_2 : SCALE_2 + 1, :] * down).astype(BF16)


def kernel_back_kernel(xwaves, gspread, tg, td, out, gs, gwaves, total):
    step = pl.program_id(0)

    @pl.when(step == 0)
    def _():
        total[...] = jnp.zeros_like(total)

    gs[...] = gspread[...].astype(F32)

    def block_of_lanes(block, carry):
        lanes = pl.ds(pl.multiple_of(LANES * block, LANES), LANES)
        square = jnp.concatenate(
            [
                jnp.concatenate(
                    [gs[r * 40 + OUT * col : r * 40 + OUT * col + OUT, lanes] for r in range(OUT)], axis=0
                ).astype(BF16)
                for col in range(TILES)
            ],
            axis=1,
        )
        gwaves[...] = dot(tg[...], square)
        for row in range(0, SLOTS, 16):
            here, there = slice(row, row + 16), slice(SLOTS + row, SLOTS + row + 16)
            sums = [total[pl.ds(SLOTS * k + row, 16), lanes] for k in range(4)]
            for col in range(TILES):
                at = slice(LANES * col, LANES * col + LANES)
                base = 2 * SLOTS * col + row
                real = xwaves[base : base + 16, lanes].astype(F32)
                imag = xwaves[base + SLOTS : base + SLOTS + 16, lanes].astype(F32)
                greal, gimag = gwaves[here, at], gwaves[there, at]
                sums = [
                    sums[0] + greal * real, sums[1] + gimag * imag, sums[2] + greal * imag, sums[3] + gimag * real
                ]
            for k in range(4):
                total[pl.ds(SLOTS * k + row, 16), lanes] = sums[k]
        return carry

    lax.fori_loop(0, 1024 // LANES, block_of_lanes, 0)

    @pl.when(step == pl.num_programs(0) - 1)
    def _():
        taps = jnp.dot(
            td[...], total[...], preferred_element_type=F32, precision=lax.Precision.HIGHEST
        )
        out[...] = jnp.concatenate([taps[:, :512], taps[:, 512:]], axis=0).astype(BF16)


def gates_back_kernel(
    near, above, own, below, left, right, glead, spec, tx, ty, gjoined, source, ext, waves, mixed_waves, ggates
):
    step = pl.program_id(0)

    @pl.when(step == 0)
    def _():
        fill(source, near, 0.0, above, own, below)
        widen(ext, slice(0, 1024), near, 0.0, source, left, right, 0, 6)

    widen(ext, slice(0, 1024), near, 0.0, source, left, right, OUT * step + 6, OUT)
    depthwise(ext, OUT * step, spec, tx, ty, waves, mixed_waves, ggates)
    gjoined[:, :128] = (ggates[:, :128] + glead[...]).astype(BF16)
    gjoined[:, 128:] = ggates[:, 128:].astype(BF16)


def in_back_kernel(
    gjoined, x_own, gmiddle, valid, vecs, in_w, grad_kernel, ffn_sums, bias_sum,
    ginput, sent, kept,
    normed_all, gjoined_all, vec_sums,
):
    step = pl.program_id(0)
    chunk = x_own.shape[0]
    rows = pl.ds(pl.multiple_of(step * chunk, 16), chunk)

    @pl.when(step == 0)
    def _():
        vec_sums[...] = jnp.zeros_like(vec_sums)

    gjoined_all[rows, :] = gjoined[...]
    gnormed = dot_right(gjoined[...], in_w[...])
    normal, inverse = normalize(x_own[...].astype(F32))
    gain = vecs[GAIN_1 : GAIN_1 + 1, :]
    mask = valid[...]
    normed_all[rows, :] = ((normal * gain + vecs[SHIFT_1 : SHIFT_1 + 1, :]) * mask).astype(BF16)
    masked = gnormed * mask
    vec_sums[0:1, :] += jnp.sum(masked * normal, axis=0, keepdims=True)
    vec_sums[1:2, :] += jnp.sum(masked, axis=0, keepdims=True)
    ginput[...] = (gmiddle[...] + norm_back(masked, normal, inverse, gain)).astype(BF16)

    @pl.when(step == pl.num_programs(0) - 1)
    def _():
        def finish(first, second):
            first[0:512, :] = dot_left(normed_all[...], gjoined_all[:, 0:512]).astype(BF16)
            block = dot_left(normed_all[...], gjoined_all[:, 512:1024]).astype(BF16)
            first[512:576, :] = block[0:64, :]
            second[0:448, :] = block[64:512, :]
            second[448:560, :] = grad_kernel[...]
            pieces = [vec_sums[0:2, :], ffn_sums[0:2, :]]
            pieces += [bias_sum[0:1, 512 * k : 512 * k + 512] for k in range(4)]
            pieces.append(jnp.zeros((8, 512), F32))
            second[560:576, :] = jnp.concatenate(pieces, axis=0).astype(BF16)

        even = lax.axis_index("col") % 2 == 0
        pl.when(even)(lambda: finish(kept, sent))
        pl.when(jnp.logical_not(even))(lambda: finish(sent, kept))


def expand_early_kernel(
    own, got, down_w, out_w, vecs,
    grad_down, grad_up, scale_2, grad_out, grad_4, grad_3, grad_2, grad_1, scale_1,
):
    step = pl.program_id(0)

    @pl.when(step == 0)
    def _():
        scale_2[...] = jnp.zeros_like(scale_2)

    def expand(first, second):
        @pl.when(step < 4)
        def _():
            block = first[...].astype(F32).T
            grad_down[...] = block
            grad_up[...] = second[...].astype(F32)
            scale_2[...] += jnp.sum(block * down_w[...].astype(F32), axis=0, keepdims=True)

        @pl.when(step == 4)
        def _():
            scale_2[...] = scale_2[...] / vecs[SCALE_2 : SCALE_2 + 1, :]
            grad_out[0:448, :] = first[0:448, :].astype(F32)
            grad_out[448:512, :] = second[0:64, :].astype(F32)
            grad_4[...] = second[64:320, :].astype(F32)
            square = second[320:448, :].astype(F32)
            grad_3[...] = square[:, 0:256]
            grad_2[...] = square[64:128, 256:384]
            grad_1[...] = square[32:64, 384 + 64 : 512]
            summed = jnp.sum(grad_out[...] * out_w[...].astype(F32), axis=0, keepdims=True)
            scale_1[...] = summed / vecs[SCALE_1 : SCALE_1 + 1, :]

    even = lax.axis_index("col") % 2 == 0
    pl.when(even)(lambda: expand(own, got))
    pl.when(jnp.logical_not(even))(lambda: expand(got, own))


def expand_late_kernel(own, got, grad_in, grad_conv, gain_1, shift_1, gain_2, shift_2, grad_bias):
    def expand(first, second):
        grad_in[:, :512] = first[:512, :].astype(F32)
        grad_in[0:64, 512:] = first[512:576, :].astype(F32)
        grad_in[64:512, 512:] = second[0:448, :].astype(F32)
        tail = second[448:576, :].astype(F32)
        taps = jnp.concatenate([tail[:56], tail[56:112]], axis=1)[:, 32:]
        for row in range(TAPS):
            grad_conv[row] = taps[TAPS * row : TAPS * row + TAPS]
        for row, ref in enumerate((gain_1, shift_1, gain_2, shift_2)):
            ref[...] = tail[112 + row : 113 + row]
        for k in range(4):
            grad_bias[:, 512 * k : 512 * k + 512] = tail[116 + k : 117 + k]

    even = lax.axis_index("col") % 2 == 0
    pl.when(even)(lambda: expand(own, got))
    pl.when(jnp.logical_not(even))(lambda: expand(got, own))


def whole(shape):
    return pl.BlockSpec(shape, lambda i: (0,) * len(shape), pipeline_mode=pl.Buffered(1))


def chunked(shape):
    return pl.BlockSpec(shape, lambda i: (i,) + (0,) * (len(shape) - 1))


def held(shape):
    return pl.BlockSpec(shape, lambda i: (0,) * len(shape))


def params(limit_mib):
    return pltpu.CompilerParams(vmem_limit_bytes=limit_mib * 1024 * 1024, dimension_semantics=("arbitrary",))


def cost(micros):
    return pl.CostEstimate(flops=int(micros * 1e10), bytes_accessed=int(micros * 3e7), transcendentals=0)


def shaped(shape, dtype):
    return jax.ShapeDtypeStruct(shape, dtype)


AXES = ("row", "col")


class Reducer:
    def __init__(self):
        self.rows = lax.axis_size("row")
        self.cols = lax.axis_size("col")
        self.row_at = lax.axis_index("row")
        self.col_at = lax.axis_index("col")
        bits = [("row", 1 << b) for b in range(self.rows.bit_length() - 1)]
        bits += [("col", 1 << b) for b in range(1, self.cols.bit_length() - 1)]
        self.steps = list(zip(bits, bits[1:-1] + [bits[0], bits[-1]]))
        self.core_step = (("col", 1), ("col", 1))
        self.core = self.col_at & 1

    def pairs(self, step):
        result = []
        for r in range(self.rows):
            for c in range(self.cols):
                axis, mask = step[c & 1]
                r2, c2 = (r ^ mask, c) if axis == "row" else (r, c ^ mask)
                result.append((r * self.cols + c, r2 * self.cols + c2))
        return result

    def bit(self, step):
        values = [((self.row_at if axis == "row" else self.col_at) & mask) != 0 for axis, mask in step]
        return jnp.where(self.core == 0, values[0], values[1]).astype(jnp.int32)

    def swap(self, block, step):
        return lax.ppermute(block, AXES, self.pairs(step))

    def open(self, sent, kept):
        return Sum(self, sent, kept)


class Sum:
    def __init__(self, reducer, sent, kept):
        self.reducer = reducer
        self.sent, self.kept, self.got = sent, kept, None
        count = len(reducer.steps)
        self.plan = [reducer.core_step] + reducer.steps + reducer.steps[-2::-1] + [reducer.core_step]
        self.halvings = count
        self.stage = 0

    @property
    def done(self):
        return self.stage == len(self.plan)

    def swap(self):
        self.got = self.reducer.swap(self.sent, self.plan[self.stage])

    def combine(self):
        sent, kept, got, stage = self.sent, self.kept, self.got, self.stage
        self.stage += 1
        self.got = None
        steps = self.reducer.steps
        if stage < self.halvings - 1:
            bit = self.reducer.bit(steps[stage])
            half = kept.shape[0] // 2

            def summed(at):
                pieces = [lax.dynamic_slice_in_dim(a, at * half, half, 0).astype(F32) for a in (kept, got)]
                return (pieces[0] + pieces[1]).astype(BF16)

            self.sent, self.kept = summed(1 - bit), summed(bit)
        elif stage <= self.halvings:
            self.sent = self.kept = (kept.astype(F32) + got.astype(F32)).astype(BF16)
        elif not self.done:
            bit = self.reducer.bit(self.plan[stage]) == 1
            self.sent = self.kept = jnp.concatenate([jnp.where(bit, got, kept), jnp.where(bit, kept, got)], axis=0)
        else:
            self.got = got

    def advance(self):
        self.swap()
        self.combine()


def shift_pairs(count):
    forward = [(i, i + 1) for i in range(count - 1)]
    return forward, [(b, a) for a, b in forward]


def on_device(
    activations, gain_first, shift_first, in_weight, conv_kernel, mix_first, mix_second, mix_third,
    mix_fourth, out_weight, scale_mixer, gain_second, shift_second, up_weight, up_bias, down_weight,
    scale_mlp, valid_pixels, tile_images, cotangent,
):
    tile_rows, tile_cols, width = activations.shape
    pixels = tile_rows * tile_cols
    hidden = up_weight.shape[1]
    gate_count = conv_kernel.shape[-1]
    joined_count = in_weight.shape[1]
    lead_count = joined_count - gate_count
    span = tile_cols + 8
    ext_rows = tile_rows + 2 * HALO
    ext_pixels = ext_rows * span
    tab = tables()
    down_pairs, up_pairs = shift_pairs(lax.axis_size("row"))
    right_pairs, left_pairs = shift_pairs(lax.axis_size("col"))

    row_at, col_at = lax.axis_index("row"), lax.axis_index("col")
    row_last, col_last = lax.axis_size("row") - 1, lax.axis_size("col") - 1
    own_image = tile_images[row_at, col_at]

    def same(row, col, inside):
        return jnp.logical_and(inside, tile_images[row, col] == own_image)

    same_up = same(jnp.maximum(row_at - 1, 0), col_at, row_at > 0)
    same_down = same(jnp.minimum(row_at + 1, row_last), col_at, row_at < row_last)
    same_left = same(row_at, jnp.maximum(col_at - 1, 0), col_at > 0)
    same_right = same(row_at, jnp.minimum(col_at + 1, col_last), col_at < col_last)

    def rows_around(block):
        return lax.ppermute(block[-HALO:], "row", down_pairs), lax.ppermute(block[:HALO], "row", up_pairs)

    def cols_around(above, below, block):
        def side(cols):
            return jnp.concatenate([above[:, cols], block[:, cols], below[:, cols]], axis=0)

        last, first = slice(tile_cols - HALO, tile_cols), slice(0, HALO)
        return lax.ppermute(side(last), "col", right_pairs), lax.ppermute(side(first), "col", left_pairs)

    near = jnp.stack([same_up, same_down, same_left, same_right]).astype(jnp.int32)

    def masked(pair, marks, outside):
        return tuple(jnp.where(mark, block, jnp.asarray(outside, BF16)) for block, mark in zip(pair, marks))

    def flat(block):
        return block.reshape(block.shape[0] * block.shape[1], block.shape[2])

    marked = jnp.where(valid_pixels[..., None] != 0, activations, jnp.asarray(OUTSIDE, BF16))
    taps = jnp.pad(conv_kernel.astype(F32).reshape(TAPS * TAPS, gate_count), ((0, 0), (lead_count, 0)))
    spec = jnp.dot(tab["spectrum"], taps, precision=lax.Precision.HIGHEST, preferred_element_type=F32)
    w1 = jnp.zeros((128, 128), BF16).at[32:64, 64:128].set(mix_first)
    w2 = jnp.zeros((128, 128), BF16).at[64:128, :].set(mix_second)
    above, below = rows_around(marked)
    (above, below, spec, w1, w2, valid_pixels) = lax.optimization_barrier(
        (above, below, spec, w1, w2, valid_pixels)
    )
    left, right = cols_around(*masked((above, below), (same_up, same_down), OUTSIDE), marked)

    x_own = activations.reshape(pixels, width)
    cot = cotangent.reshape(pixels, width)
    valid = valid_pixels.astype(F32).reshape(pixels, 1)
    vecs = jnp.stack(
        [gain_first, shift_first, scale_mixer, gain_second, shift_second, scale_mlp, scale_mlp, scale_mlp]
    ).astype(F32)
    bias = up_bias.astype(F32).reshape(1, hidden)
    w3, w4 = mix_third, mix_fourth
    (left, right, valid, vecs, bias) = lax.optimization_barrier((left, right, valid, vecs, bias))
    x_source = flat(above), flat(marked), flat(below), left, right

    chunk = OUT * tile_cols
    steps = tile_rows // OUT
    anywhere = pl.BlockSpec(memory_space=pl.ANY)
    in_smem = pl.BlockSpec(memory_space=pltpu.SMEM)
    rows = 256
    count = pixels // rows
    wide = 640
    few = pixels // wide
    early = hidden + width
    late = 576
    dma = pltpu.SemaphoreType.DMA
    (
        xwaves, spread, prods, lead, middle, active, gmiddle, ffn_sent, ffn_kept, ffn_sums, bias_sum,
    ) = pl.pallas_call(
        forward_kernel,
        grid=(steps,),
        in_specs=[
            in_smem,
            chunked((chunk, width)), whole((pixels, 1)), whole((pixels, width)), whole((8, width)),
            whole((1, hidden)), whole((128, 128)), whole((128, 128)), whole(w3.shape), whole(tab["window"].shape),
            whole(tab["tile_back"].shape),
            whole((HALO * tile_cols, width)), whole((pixels, width)), whole((HALO * tile_cols, width)),
            whole((ext_rows, HALO, width)), whole((ext_rows, HALO, width)),
        ] + [anywhere] * 6,
        out_specs=[anywhere, anywhere, anywhere, chunked((chunk, 128))] + [anywhere] * 5 + [
            held((8, width)), held((8, hidden)),
        ],
        out_shape=[
            shaped((steps * 2 * SLOTS * TILES, joined_count), BF16), shaped((pixels, joined_count), F32),
            shaped((pixels, joined_count), F32), shaped((pixels, 128), F32),
            shaped((pixels, width), F32), shaped((pixels, hidden), BF16), shaped((pixels, width), F32),
            shaped((early, width), BF16), shaped((early, width), BF16), shaped((8, width), F32),
            shaped((8, hidden), F32),
        ],
        scratch_shapes=[
            pltpu.VMEM((ext_pixels, joined_count + 128), F32),
            pltpu.VMEM((2 * SLOTS, LANES * TILES), F32), pltpu.VMEM((2 * SLOTS, LANES * TILES), BF16),
            pltpu.VMEM((pixels, hidden), BF16), pltpu.VMEM((pixels, width), BF16), pltpu.VMEM((pixels, width), BF16),
            pltpu.VMEM((pixels, hidden), BF16), pltpu.VMEM((pixels, width), F32),
            pltpu.VMEM((ext_rows * tile_cols, width), F32), pltpu.VMEM((ext_pixels, width), F32),
            pltpu.VMEM((width, joined_count), BF16),
            pltpu.VMEM((3 * SLOTS, joined_count), F32), pltpu.VMEM(w4.shape, BF16), pltpu.VMEM((width, width), BF16),
            pltpu.VMEM((width, hidden), BF16), pltpu.VMEM((hidden, width), BF16),
            pltpu.VMEM((2 * SLOTS * TILES, joined_count), BF16),
            pltpu.VMEM((chunk, joined_count), F32), pltpu.VMEM((chunk, joined_count), F32),
            pltpu.VMEM((hidden, width), BF16), pltpu.VMEM((hidden, width), BF16),
            dma((6,)), dma((steps,)), dma((steps,)), dma((steps,)), dma((steps,)), dma((steps,)), dma((2,)),
            dma((4,)), dma((4,)),
        ],
        compiler_params=params(62),
        cost_estimate=cost(45),
        name="forward",
    )(
        near, x_own, valid, cot, vecs, bias, w1, w2, w3, tab["window"], tab["tile_back"],
        *x_source, in_weight, spec, w4, out_weight, up_weight, down_weight,
    )

    gspread, glead, ffn_sent, ffn_kept = pl.pallas_call(
        mixer_back_kernel,
        grid=(few,),
        in_specs=[
            chunked((wide, width)), chunked((wide, joined_count)), chunked((wide, joined_count)),
            chunked((wide, 128)), whole((8, width)), whole((128, 128)), whole((128, 128)), whole(w3.shape),
            whole(w4.shape), whole((width, width)), anywhere, anywhere,
        ],
        out_specs=[chunked((wide, joined_count)), chunked((wide, 128)), anywhere, anywhere],
        out_shape=[
            shaped((pixels, joined_count), BF16), shaped((pixels, 128), F32), shaped((early, width), BF16),
            shaped((early, width), BF16),
        ],
        input_output_aliases={10: 2, 11: 3},
        scratch_shapes=[
            pltpu.VMEM((width, width), F32), pltpu.VMEM(w4.shape, F32), pltpu.VMEM(w3.shape, F32),
            pltpu.VMEM((128, 128), F32), pltpu.VMEM((128, 128), F32), pltpu.VMEM((2 * width, width), BF16),
            pltpu.SemaphoreType.DMA((2,)),
        ],
        compiler_params=params(48),
        cost_estimate=cost(9),
        name="mixer_back",
    )(gmiddle, spread, prods, lead, vecs, w1, w2, w3, w4, out_weight, ffn_sent, ffn_kept)

    reducer = Reducer()
    ffn = reducer.open(ffn_sent, ffn_kept)
    ffn.swap()
    tie = lax.optimization_barrier
    block = gspread.reshape(tile_rows, tile_cols, joined_count)
    above, below = rows_around(block)
    ffn.combine()
    (gspread, ffn.sent, ffn.kept) = tie((gspread, ffn.sent, ffn.kept))
    grad_kernel = pl.pallas_call(
        kernel_back_kernel,
        grid=(steps,),
        in_specs=[
            chunked((2 * SLOTS * TILES, joined_count)), chunked((chunk, joined_count)),
            whole(tab["tile"].shape), whole(tab["kernel_back"].shape),
        ],
        out_specs=held((112, width)),
        out_shape=shaped((112, width), BF16),
        scratch_shapes=[
            pltpu.VMEM((chunk, joined_count), F32), pltpu.VMEM((2 * SLOTS, LANES * TILES), F32),
            pltpu.VMEM((4 * SLOTS, joined_count), F32),
        ],
        compiler_params=params(48),
        cost_estimate=cost(9),
        name="kernel_back",
    )(xwaves, gspread, tab["tile"], tab["kernel_back"])
    (above, below, grad_kernel, ffn.sent) = tie((above, below, grad_kernel, ffn.sent))
    ffn.swap()
    left, right = cols_around(*masked((above, below), (same_up, same_down), 0.0), block)
    above, below = flat(above), flat(below)

    gjoined = pl.pallas_call(
        gates_back_kernel,
        grid=(steps,),
        in_specs=[
            in_smem,
            whole((HALO * tile_cols, joined_count)), whole((pixels, joined_count)),
            whole((HALO * tile_cols, joined_count)), whole((ext_rows, HALO, joined_count)),
            whole((ext_rows, HALO, joined_count)), chunked((chunk, 128)),
            pl.BlockSpec((3 * SLOTS, joined_count), lambda i: (1, 0), pipeline_mode=pl.Buffered(1)),
            whole(tab["window"].shape), whole(tab["tile_back"].shape),
        ],
        out_specs=chunked((chunk, joined_count)),
        out_shape=shaped((pixels, joined_count), BF16),
        scratch_shapes=[
            pltpu.VMEM((ext_rows * tile_cols, joined_count), F32), pltpu.VMEM((ext_pixels, joined_count), F32), pltpu.VMEM((2 * SLOTS, LANES * TILES), F32),
            pltpu.VMEM((2 * SLOTS, LANES * TILES), BF16), pltpu.VMEM((chunk, joined_count), F32),
        ],
        compiler_params=params(48),
        cost_estimate=cost(11),
        name="gates_back",
    )(near, above, gspread, below, left, right, glead, spec, tab["window"], tab["tile_back"])
    (gjoined, ffn.got) = tie((gjoined, ffn.got))
    ffn.combine()
    (gjoined, ffn.sent, ffn.kept) = tie((gjoined, ffn.sent, ffn.kept))
    ffn.swap()

    ginput, rest_sent, rest_kept = pl.pallas_call(
        in_back_kernel,
        grid=(few,),
        in_specs=[
            chunked((wide, joined_count)), chunked((wide, width)), chunked((wide, width)), chunked((wide, 1)),
            whole((8, width)), whole((width, joined_count)), whole((112, width)),
            whole((8, width)), whole((8, hidden)),
        ],
        out_specs=[chunked((wide, width)), held((late, width)), held((late, width))],
        out_shape=[
            shaped((pixels, width), BF16), shaped((late, width), BF16), shaped((late, width), BF16),
        ],
        scratch_shapes=[
            pltpu.VMEM((pixels, width), BF16), pltpu.VMEM((pixels, joined_count), BF16), pltpu.VMEM((8, width), F32),
        ],
        compiler_params=params(24),
        cost_estimate=cost(8),
        name="in_back",
    )(
        gjoined, x_own, gmiddle, valid, vecs, in_weight, grad_kernel, ffn_sums, bias_sum,
    )
    rest = reducer.open(rest_sent, rest_kept)
    rest.swap()
    (rest.kept, ffn.got) = tie((rest.kept, ffn.got))
    ffn.combine()
    ffn.swap()

    def down(active, before, first, blocks):
        return pl.pallas_call(
            down_kernel,
            grid=(blocks,),
            in_specs=[
                pl.BlockSpec((rows, hidden), lambda i: (i + first, 0)),
                pl.BlockSpec((rows, width), lambda i: (i + first, 0)), whole((8, width)), whole((hidden, width)),
                pl.BlockSpec(memory_space=pl.ANY),
            ],
            out_specs=pl.BlockSpec((rows, width), lambda i: (i + first, 0)),
            out_shape=shaped((pixels, width), BF16),
            input_output_aliases={4: 0} if first else {},
            compiler_params=params(12),
            cost_estimate=cost(4),
            name="down",
        )(active, middle, vecs, down_weight, before)

    (active, rest.sent, ffn.sent) = tie((active, rest.sent, ffn.sent))
    outputs = down(active, jnp.zeros((8, 128), BF16), 0, count // 2)

    def onward(way, *others):
        values = tie((way.kept, way.got) + others)
        way.kept, way.got = values[:2]
        way.combine()
        if not way.done:
            way.swap()
        return values[2:]

    (outputs,) = onward(rest, outputs)
    (rest.kept,) = onward(ffn, rest.kept)
    (outputs, rest.sent, ffn.sent) = tie((outputs, rest.sent, ffn.sent))
    outputs = down(active, outputs, count // 2, count - count // 2)
    (outputs,) = onward(rest, outputs)
    vector = shaped((1, width), F32)
    block_at = lambda i: (jnp.minimum(i, 3), 0)
    expand_early = pl.pallas_call(
        expand_early_kernel,
        grid=(5,),
        in_specs=[
            chunked((width, width)), chunked((width, width)), pl.BlockSpec((width, width), block_at),
            whole((width, width)), whole((8, width)),
        ],
        out_specs=[
            pl.BlockSpec((width, width), block_at), pl.BlockSpec((width, width), lambda i: (0, jnp.minimum(i, 3))),
            held((1, width)), held((width, width)), held(w4.shape), held(w3.shape), held(mix_second.shape),
            held(mix_first.shape), held((1, width)),
        ],
        out_shape=[
            shaped((hidden, width), F32), shaped((width, hidden), F32), vector, shaped((width, width), F32),
            shaped(w4.shape, F32), shaped(w3.shape, F32), shaped(mix_second.shape, F32),
            shaped(mix_first.shape, F32), vector,
        ],
        compiler_params=params(32),
        cost_estimate=cost(5),
        name="expand_early",
    )
    expanded = None
    for who in "frfrfrrrfrfr":
        way, other = (ffn, rest) if who == "f" else (rest, ffn)
        if not way.done:
            (other.kept,) = onward(way, other.kept)
        if ffn.done and expanded is None:
            expanded = expand_early(ffn.kept, ffn.got, down_weight, out_weight, vecs)
            (rest.kept, expanded) = tie((rest.kept, expanded))
    while not (ffn.done and rest.done):
        for way in (ffn, rest):
            if not way.done:
                onward(way)
    if expanded is None:
        expanded = expand_early(ffn.kept, ffn.got, down_weight, out_weight, vecs)
    (grad_down_weight, grad_up_weight, scale_2, grad_out, grad_4, grad_3, grad_2, grad_1, scale_1) = expanded
    grad_in_weight, grad_conv, gain_1, shift_1, gain_2, shift_2, grad_bias = pl.pallas_call(
        expand_late_kernel,
        in_specs=[pl.BlockSpec(memory_space=pltpu.VMEM)] * 2,
        out_specs=[pl.BlockSpec(memory_space=pltpu.VMEM)] * 7,
        out_shape=[
            shaped(in_weight.shape, F32), shaped(conv_kernel.shape, F32), vector, vector, vector, vector,
            shaped((1, hidden), F32),
        ],
        compiler_params=pltpu.CompilerParams(vmem_limit_bytes=32 * 1024 * 1024),
        cost_estimate=cost(3),
        name="expand_late",
    )(rest.kept, rest.got)
    return (
        outputs.reshape(activations.shape),
        ginput.reshape(activations.shape),
        gain_1.reshape(width),
        shift_1.reshape(width),
        grad_in_weight,
        grad_conv,
        grad_1,
        grad_2,
        grad_3,
        grad_4,
        grad_out,
        scale_1.reshape(width),
        gain_2.reshape(width),
        shift_2.reshape(width),
        grad_up_weight,
        grad_bias.reshape(hidden),
        grad_down_weight,
        scale_2.reshape(width),
    )


def solution(mesh):
    tiles = P("row", "col", None)
    in_specs = (tiles,) + (P(),) * 16 + (P("row", "col"), P(), tiles)
    out_specs = (tiles, tiles) + (P(),) * 16
    return jax.shard_map(on_device, mesh=mesh, in_specs=in_specs, out_specs=out_specs, check_vma=False)
```
